512 devices in a mesh: freq: 2 (over x_hi), grp: 16 (over z), sub: 16 (over y, x_lo, core).
Axes of the slice: x: 4 (x_hi: 2, x_lo: 2; x = x_hi * 2 + x_lo), y: 4, z: 16, core: 2. Of those that a mesh axis runs over, the one named last changes fastest.
Arguments:
- alm: bfloat16 [256, 256, 2, 1024], P('freq', ('grp', 'sub')), may hold values from -6 to 6
- band_index: int32 [32, 32], replicated, may hold values from 0 to 255
- band_weight: float32 [32, 32], replicated, may hold values from 0.05 to 0.5
- legendre: bfloat16 [256, 1024, 1024], P(('grp', 'sub')), may hold values from -0.0078125 to 0.0078125
- orders: int32 [256], replicated, may hold values from 0 to 1023, as said below
- owner: int32 [524288, 1], P(('grp', 'sub')), may hold values from 0 to 255; in each aligned block of 2048 rows (0 to 2047, 2048 to 4095, ...) at most 12 rows name the same one
- tile_local: int32 [524288], P(('grp', 'sub')), may hold values from 0 to 7
- interp: bfloat16 [524288, 512], P(('grp', 'sub')), may hold values from -0.25 to 0.25
Outputs:
- tod: bfloat16 [524288, 32], P(('grp', 'sub'), 'freq')
The draws below stay inside these ranges and needn't reach their ends.
Inputs may be any that keep to these rules, and one draw needn't show every extreme that they name: 256 distinct orders; 0 and 1023 are always among them. `owner`: among the 2048 samples of one index of grp and sub (aligned blocks of 2048 rows) no cycle band is named more than 12 times, a bound that some block reaches.
All inputs are finite; a program needn't handle non-finite values.
Results may differ from the reference program's by a relative error of at most 0.0073.
Values may be sent and summed in bfloat16 or wider, within the bound.
A program may use at most 64 MiB of HBM per device.

```python
import math
import jax
import jax.numpy as jnp
import numpy as np
from jax import lax

FREQS = 256
DET = 32
K = 32
L = 1024
R = 1024
NPHI = 1024
TR = 4
TPHI = 128
SD = 2048
OWNERS = 256
M = 256
NT_DEV = 8
TPIX = 512
CAP = 12
S = 524288


def draw_orders(key, part):
    first_key, second_key = jax.random.split(jax.random.fold_in(key, 11))
    middle = jax.random.permutation(first_key, L - 2)[:M - 2] + 1
    values = jnp.concatenate([jnp.zeros((1,), jnp.int32), jnp.full((1,), L - 1, jnp.int32), middle.astype(jnp.int32)])
    return jax.random.permutation(second_key, values)


def plant(drawn, stream_key, smallest, largest):
    index_at = [jax.random.randint(jax.random.fold_in(stream_key, axis), (), 0, length) for axis, length in enumerate(drawn.shape)]
    longest = drawn.shape.index(max(drawn.shape))
    next_to = index_at[:longest] + [(index_at[longest] + 1) % drawn.shape[longest]] + index_at[longest + 1:]
    return drawn.at[tuple(index_at)].set(smallest).at[tuple(next_to)].set(largest)


def level_of(own_key, dims, cuts, least, largest):
    gain, own = 1.0, jax.random.fold_in(own_key, 6)
    for dim, blocks in cuts:
        heights = jnp.exp(jax.random.uniform(jax.random.fold_in(own, dim), (blocks,), jnp.float32, least / len(cuts), largest / len(cuts)))
        gain = gain * jnp.repeat(heights, dims[dim] // blocks).reshape([-1 if axis == dim else 1 for axis in range(len(dims))])
    return gain


def assign_block(rng, own, number, rows, count, top, limit, lean):
    ranking = jax.random.permutation(rng, count)
    heavy_load, usual = shares(count, rows * top, limit, lean, True), shares(count, rows * top, limit, lean, False)
    places = jnp.arange(count)

    def named(tallies, turn):
        used = int((tallies > 0).sum())
        fixed = max(1, used // 4)
        passed = fixed + (places - fixed + turn * (used - fixed)) % max(1, count - fixed)
        return jnp.zeros((count,), jnp.int32).at[ranking[jnp.where(places < fixed, places, passed)]].set(jnp.asarray(tallies, jnp.int32))

    tallies = jnp.where(number % 4 == 0, named(heavy_load, number // 4), named(usual, number - number // 4 - 1))
    mixed = jax.random.permutation(jax.random.fold_in(own, 3), count)
    donor, sink = mixed[0:count // 2 * 2:2], mixed[1:count // 2 * 2:2]
    margin = jnp.minimum(tallies[donor] - 1, limit - tallies[sink]) // 2
    margin = jnp.where((donor == ranking[0]) | (sink == ranking[0]) | (tallies[sink] == 0), 0, jnp.maximum(margin, 0))
    passed = jax.random.randint(jax.random.fold_in(own, 4), (count // 2,), 0, 1 << 20) % (margin + 1)
    tallies = tallies.at[donor].add(-passed).at[sink].add(passed)
    labels = jnp.searchsorted(jnp.cumsum(tallies), jnp.arange(rows * top), side="right").astype(jnp.int32)
    listing = labels.reshape(top, rows).T
    listing = listing[jax.random.permutation(jax.random.fold_in(own, 1), rows)]
    turn = jax.random.randint(jax.random.fold_in(own, 2), (rows, 1), 0, top)
    return jnp.take_along_axis(listing, (jnp.arange(top)[None, :] + turn) % top, axis=1)


def shares(amount, total, limit, skew, full):
    portions = [(1 << 20) // math.isqrt(standing ** skew) + 1 for standing in range(1, amount + 1)]
    largest = limit if full else min(limit, max(-(-total // amount), total * portions[0] // sum(portions)))
    least = 1 if total - largest >= amount - 1 else 0
    holding, rest = [largest] + [least] * (amount - 1), total - largest - least * (amount - 1)
    while rest > 0:
        free = [i for i in range(1, amount) if holding[i] < largest] or [i for i in range(1, amount) if holding[i] < limit]
        whole, budget = sum([portions[i] for i in free]), rest
        for i in free:
            more = min(limit - holding[i], max(1, budget * portions[i] // whole), rest)
            holding[i] = holding[i] + more
            rest = rest - more
    return np.array(holding)


def gaussian(own_key, extent, scale, bound, cuts=(), held_as=jnp.bfloat16):
    array = scale * jax.random.normal(own_key, extent, jnp.float32)
    if cuts:
        array = array * level_of(own_key, extent, cuts, -0.22, 0.18)
    return jnp.clip(array, -bound, bound).astype(held_as)


def setup_inputs(seed: int = 0) -> dict:
    streams_of = jax.random.split(jax.random.key(seed), 9)
    alm = gaussian(streams_of[0], (FREQS, M, 2, L), 1.0, 6.0, ((0, 2), (1, 256)))
    band_index = plant(jax.random.randint(streams_of[1], (DET, K), 0, FREQS), jax.random.fold_in(streams_of[1], 1), 0, FREQS - 1).astype(jnp.int32)
    band_weight = jnp.clip(jnp.exp(jax.random.uniform(streams_of[2], (DET, K), jnp.float32, math.log(0.05), math.log(0.5))), 0.05, 0.5)
    legendre = gaussian(streams_of[3], (M, L, R), (2 * L * M) ** -0.5, 0.0078125, ((0, 256),))
    orders = draw_orders(jax.random.fold_in(streams_of[8], 71), 0)
    owner_keys = jax.random.split(jax.random.fold_in(streams_of[5], 1), S // SD)
    owner_turns = jax.random.permutation(jax.random.fold_in(streams_of[5], 3), S // SD)
    owner = jax.vmap(lambda own, number: assign_block(jax.random.fold_in(streams_of[5], 2), own, number, SD, OWNERS, 1, CAP, 2))(owner_keys, owner_turns).reshape((S, 1))
    tile_local = plant(jax.random.randint(streams_of[6], (S,), 0, NT_DEV), jax.random.fold_in(streams_of[6], 1), 0, NT_DEV - 1).astype(jnp.int32)
    interp = gaussian(streams_of[7], (S, TPIX), TPIX ** -0.5, 0.25, ((0, 256),))
    return dict(alm=alm, band_index=band_index, band_weight=band_weight, legendre=legendre, orders=orders, owner=owner, tile_local=tile_local, interp=interp)


def band_matrix(band_index, band_weight, first_freq, freq_count):
    freq_ids = first_freq + lax.iota(jnp.int32, freq_count)
    matches = (band_index[:, :, None] == freq_ids[None, None, :]).astype(jnp.float32)
    return jnp.sum(matches * band_weight[:, :, None], axis=1).astype(jnp.bfloat16)


def phase_basis(order_list, longitudes):
    lon_index = lax.iota(jnp.int32, longitudes)
    phase_turns = (order_list[:, None] * lon_index[None, :]) % longitudes
    angles = phase_turns.astype(jnp.float32) * (2.0 * math.pi / longitudes)
    factor = jnp.where(order_list == 0, 1.0, 2.0).astype(jnp.float32)[:, None]
    return jnp.stack([factor * jnp.cos(angles), -factor * jnp.sin(angles)]).astype(jnp.bfloat16)


def reference(alm, band_index, band_weight, legendre, orders, owner, tile_local, interp):
    band_full = band_matrix(band_index, band_weight, 0, FREQS)
    flat_alm = alm.reshape(FREQS, M * 2 * L)
    detector_alm = jnp.dot(band_full, flat_alm, preferred_element_type=jnp.float32).astype(jnp.bfloat16)
    detector_alm = detector_alm.reshape(DET, M, 2, L)
    degree = lax.iota(jnp.int32, L)

    def one_order(member):
        coefs, table, order_value = member
        panel = jnp.where(degree[:, None] >= order_value, table, jnp.zeros_like(table))
        result = jnp.dot(coefs.reshape(DET * 2, L), panel, preferred_element_type=jnp.float32)
        return result.astype(jnp.bfloat16).reshape(DET, 2, R)

    cycle_coef = lax.map(one_order, (jnp.transpose(detector_alm, (1, 0, 2, 3)), legendre, orders))
    basis = phase_basis(orders, NPHI)
    sky = jnp.einsum("mdcr,cmj->drj", cycle_coef.astype(jnp.float32), basis.astype(jnp.float32))
    sky = sky.astype(jnp.bfloat16)
    cycle_tiles = R // TR
    lon_tiles = NPHI // TPHI
    tiles = sky.reshape(DET, cycle_tiles, TR, lon_tiles, TPHI).transpose(1, 3, 0, 2, 4)
    tiles = tiles.reshape(cycle_tiles * lon_tiles, DET, TR * TPHI)
    global_tile = owner[:, 0] * NT_DEV + tile_local
    block_rows = min(1024, S)
    if S % block_rows != 0:
        block_rows = S

    def one_block(member):
        weights, tile_ids = member
        picked = tiles[tile_ids].astype(jnp.float32)
        return jnp.einsum("bp,bdp->bd", weights.astype(jnp.float32), picked).astype(jnp.bfloat16)

    tod = lax.map(one_block, (interp.reshape(S // block_rows, block_rows, TR * TPHI), global_tile.reshape(S // block_rows, block_rows)))
    return tod.reshape(S, DET)
```

```python
import math

import jax
import jax.numpy as jnp
import numpy as np
from jax import lax
from jax.experimental import pallas as pl
from jax.experimental.pallas import tpu as pltpu
from jax.sharding import PartitionSpec as P

MESH = pl.DeviceIdType.MESH
F32, BF16, I32 = jnp.float32, jnp.bfloat16, jnp.int32
NF, NG, NS = 2, 16, 16
DET = 32
HALF_DET = DET // NF
L = 1024
RH = 512
NPHI = 1024
SD = 2048
PIX = 512
CAP = 12
NJ = 8
ROWS = NJ * CAP
GROUP = ROWS // 2
HALF_LANES = NS * GROUP
LANES = 2 * HALF_LANES
NN = (((1,), (0,)), ((), ()))
NT = (((1,), (1,)), ((), ()))
TN = (((0,), (0,)), ((), ()))


def dot(a, b, dims=NN):
    return lax.dot_general(a, b, dims, preferred_element_type=F32)


def lane_table():
    lane = np.arange(LANES)
    g, rest = lane // HALF_LANES, lane % HALF_LANES
    s, j4, k = rest // GROUP, rest % GROUP // CAP, rest % CAP
    table = np.zeros((8, LANES), np.int32)
    table[0] = s * NJ + g * 4 + j4
    table[1] = k
    table[2] = g * 4 + j4
    table[3] = s * 16 + k
    table[4] = j4 * 8
    return table


def kernel(
    order_ref, part_ref, leg_ref, int_ref, own_ref, tile_ref, ordb_ref, tab_ref, out_ref,
    part_s, part_r, leg_v, int_v, pick, d_s, d_r, y_s, y_r, y_f, coef, basis, acc, tiles,
    v_s, v_r, cols, sel_v, sel_s, rank_v,
    loc_sem, ex_sem, ys_sem, yr_sem, ds_sem, dr_sem, rs_sem, rr_sem, vs_sem, vr_sem,
):
    f, z, s = lax.axis_index("freq"), lax.axis_index("grp"), lax.axis_index("sub")
    me = f * NS + s

    leg_copy = pltpu.make_async_copy(
        leg_ref.at[0, :, pl.ds(pl.multiple_of(f * RH, RH), RH)], leg_v, loc_sem.at[0]
    )
    int_copy = pltpu.make_async_copy(int_ref, int_v, loc_sem.at[1])
    leg_copy.start()
    int_copy.start()

    barrier = pltpu.get_barrier_semaphore()

    def greet(k, _):
        other = lax.rem(me + k, NF * NS)
        pl.semaphore_signal(
            barrier, inc=1, device_id=(other // NS, z, lax.rem(other, NS)), device_id_type=MESH
        )
        return 0

    lax.fori_loop(1, NF * NS, greet, 0)
    up, down = lax.rem(z + 1, NG), lax.rem(z + NG - 1, NG)
    for zz in (up, down):
        pl.semaphore_signal(barrier, inc=1, device_id=(f, zz, s), device_id_type=MESH)
    part_s[...] = part_ref[...].astype(BF16)
    pl.semaphore_wait(barrier, NF * NS - 1 + 2)

    exchange = pltpu.make_async_remote_copy(
        src_ref=part_s, dst_ref=part_r, send_sem=ex_sem.at[0], recv_sem=ex_sem.at[1],
        device_id=(1 - f, z, s), device_id_type=MESH,
    )
    exchange.start()

    lane = lax.broadcasted_iota(I32, (128, 128), 1)
    row = lax.broadcasted_iota(I32, (128, 128), 0)
    before = (row < lane).astype(BF16)
    band_row = lax.broadcasted_iota(I32, (NF * NS * NJ, 128), 0)
    rank_row = lax.broadcasted_iota(I32, (16, 128), 0)
    seen = jnp.zeros((NF * NS * NJ, 1), F32)
    slot_tile = jnp.zeros((16, NF * NS * NJ), F32)
    for c in range(SD // 128):
        named = band_row == own_ref[c : c + 1, :]
        ones = jnp.where(named, 1.0, 0.0)
        marks = ones.astype(BF16)
        count = dot(marks, before) + seen
        rank = jnp.sum(jnp.where(named, count, 0.0), axis=0, keepdims=True)
        seen = seen + jnp.sum(ones, axis=1, keepdims=True)
        rank_i = rank.astype(I32)
        rank_v[c : c + 1, :] = rank_i
        ids = jnp.where(rank_row == rank_i, tile_ref[c : c + 1, :].astype(F32), 0.0)
        slot_tile = slot_tile + dot(ids.astype(BF16), marks, NT)
    half_tile = jnp.where(f == 0, slot_tile[:, :128], slot_tile[:, 128:])
    lane16 = lax.broadcasted_iota(I32, (16, 128), 1)
    mine16 = lane16 // NJ == s

    def put_tiles(other, _):
        turned = pltpu.roll(half_tile, lax.rem(s - other + NS, NS) * NJ, 1)
        y_s[other, 16:32, :] = jnp.where(mine16, turned, 0.0).astype(BF16)
        return 0

    lax.fori_loop(0, NS, put_tiles, 0)

    int_copy.wait()
    slot_row = lax.broadcasted_iota(I32, (4 * ROWS, 128), 0)

    def pack(q, _):
        wanted = slot_row + q * (4 * ROWS)
        for c in range(SD // 128):
            key = (own_ref[c : c + 1, :] - f * 128) * CAP + rank_v[c : c + 1, :]
            pick[:, c * 128 : (c + 1) * 128] = jnp.where(wanted == key, 1.0, 0.0).astype(BF16)
        packed = dot(pick[...], int_v[...]).astype(BF16)
        for n in range(4):
            d_s[q * 4 + n] = packed[n * ROWS : (n + 1) * ROWS, :]
        return 0

    lax.fori_loop(0, 4, pack, 0)

    exchange.wait_recv()
    total = part_ref[...] + part_r[...].astype(F32)
    degree = lax.rem(lax.broadcasted_iota(I32, (DET, 2 * L), 1), L)
    total = jnp.where(degree >= order_ref[z * NS + s], total, 0.0).astype(BF16)
    leg_copy.wait()
    cyc = dot(jnp.concatenate([total[:, :L], total[:, L:]], axis=0), leg_v[...])
    turn = lax.broadcasted_iota(I32, (DET, RH), 1) & 3
    quads = (
        lax.broadcasted_iota(I32, (128, RH), 1) // 4 == lax.broadcasted_iota(I32, (128, RH), 0)
    ).astype(BF16)
    halves = []
    for c in range(2):
        one = cyc[c * DET : (c + 1) * DET, :]
        spread = jnp.concatenate([jnp.where(turn == i, one, 0.0) for i in range(4)], axis=0)
        halves.append(dot(quads, spread.astype(BF16), NT).reshape(NS, NJ, 128))
    y_s[:, 0:16, :] = jnp.concatenate(halves, axis=1).astype(BF16)

    def y_copy(k, dst):
        return pltpu.make_async_remote_copy(
            src_ref=y_s.at[lax.rem(s + k, NS)], dst_ref=y_r.at[dst],
            send_sem=ys_sem.at[k], recv_sem=yr_sem.at[k],
            device_id=(f, z, lax.rem(s + k, NS)), device_id_type=MESH,
        )

    def d_copy(k, dst):
        return pltpu.make_async_remote_copy(
            src_ref=d_s.at[lax.rem(s + k, NS)], dst_ref=d_r.at[dst],
            send_sem=ds_sem.at[k], recv_sem=dr_sem.at[k],
            device_id=(f, z, lax.rem(s + k, NS)), device_id_type=MESH,
        )

    def start_y(k, _):
        y_copy(k, s).start()
        return 0

    def start_d(k, _):
        d_copy(k, s).start()
        return 0

    lax.fori_loop(1, NS, start_y, 0)
    lax.fori_loop(1, NS, start_d, 0)
    y_r[s] = y_s[s]
    d_r[s] = d_s[s]

    def make_basis(p, _):
        hops = (p + 1) // 2
        zz = lax.rem(z + NG + (1 - 2 * lax.rem(p, 2)) * hops, NG)
        orders = ordb_ref[pl.ds(pl.multiple_of(zz * NS, NS), NS), :]
        lon = lax.broadcasted_iota(I32, (NS, 128), 1)
        fine = ((orders * lon) & (NPHI - 1)).astype(F32) * (2.0 * math.pi / NPHI)
        coarse = ((orders * (lon * 128)) & (NPHI - 1)).astype(F32) * (2.0 * math.pi / NPHI)
        weight = jnp.where(orders == 0, 1.0, 2.0)
        cos_u, sin_u = weight * jnp.cos(fine), weight * jnp.sin(fine)
        cos_t, sin_t = jnp.cos(coarse), jnp.sin(coarse)
        top = pl.multiple_of(p * 32, 32)
        for t in range(8):
            ct, st = cos_t[:, t : t + 1], sin_t[:, t : t + 1]
            basis[pl.ds(top, NS), t * 128 : (t + 1) * 128] = (ct * cos_u - st * sin_u).astype(BF16)
            basis[pl.ds(top + NS, NS), t * 128 : (t + 1) * 128] = (-(st * cos_u + ct * sin_u)).astype(BF16)
        return 0

    lax.fori_loop(0, NG, make_basis, 0)

    sel_s[...] = (lax.broadcasted_iota(I32, (256, LANES), 0) == tab_ref[3:4, :]).astype(BF16)
    cols[...] = jnp.zeros_like(cols)
    cols[0:16, :] = ((own_ref[...] // NJ) * 16 + rank_v[...]).astype(F32)
    cols[16:32, :] = (own_ref[...] & (NJ - 1)).astype(F32)
    turned_cols = cols[...].T
    place = lax.broadcasted_iota(I32, (128, NF * NS * 16), 1).astype(F32)
    for c in range(SD // 128):
        sel_v[c * 128 : (c + 1) * 128, :] = (place == turned_cols[:, c : c + 1]).astype(BF16)

    def wait_y(k, _):
        y_copy(k, lax.rem(s + NS - k, NS)).wait_recv()
        return 0

    lax.fori_loop(1, NS, wait_y, 0)
    y_f[...] = y_r[:, 0:16, :].astype(F32).reshape(NS * 16, 128)
    for c in range(2):
        for j in range(NJ):
            coef[c * 16 : (c + 1) * 16, j * 128 : (j + 1) * 128] = y_f[
                pl.ds(c * NJ + j, NS, stride=16), :
            ].astype(BF16)

    def ring(k, way):
        source = 0 if k == 1 else 2 * (k - 1) - (way == 0)
        target = 2 * k - (way == 0)
        return pltpu.make_async_remote_copy(
            src_ref=coef.at[pl.ds(source * 32, 32), :], dst_ref=coef.at[pl.ds(target * 32, 32), :],
            send_sem=rs_sem.at[target], recv_sem=rr_sem.at[target],
            device_id=(f, up if way == 0 else down, s), device_id_type=MESH,
        )

    def sky_first(j, _):
        at = pl.multiple_of(j * 128, 128)
        acc[pl.ds(at, 128), :] = dot(coef[0:256, pl.ds(at, 128)], basis[0:256, :], TN)
        return 0

    for k in range(1, 9):
        ways = (0, 1) if k < 8 else (0,)
        for way in ways:
            ring(k, way).start()
        if k >= 5:
            lax.fori_loop((k - 5) * 2, (k - 4) * 2, sky_first, 0)
        for way in ways:
            ring(k, way).wait_recv()

    def sky_last(j, _):
        at = pl.multiple_of(j * 128, 128)
        sky = acc[pl.ds(at, 128), :] + dot(coef[256:512, pl.ds(at, 128)], basis[256:512, :], TN)
        sky = sky.astype(BF16)
        for i in range(4):
            for t in range(8):
                tiles[j, t * DET : (t + 1) * DET, i * 128 : (i + 1) * 128] = sky[
                    i * DET : (i + 1) * DET, t * 128 : (t + 1) * 128
                ]
        return 0

    lax.fori_loop(0, NJ, sky_last, 0)

    tile_sum = jnp.sum(y_r[:, 16:32, :].astype(F32), axis=0).astype(BF16)
    here = (lax.broadcasted_iota(I32, (128, LANES), 0) == tab_ref[0:1, :]).astype(BF16)
    by_rank = dot(tile_sum, here)
    own_rank = lax.broadcasted_iota(I32, (16, LANES), 0) == tab_ref[1:2, :]
    code = jnp.sum(jnp.where(own_rank, by_rank, 0.0), axis=0, keepdims=True).astype(I32)
    code = code + tab_ref[4:5, :]

    def wait_d(k, _):
        d_copy(k, lax.rem(s + NS - k, NS)).wait_recv()
        return 0

    lax.fori_loop(1, NS, wait_d, 0)
    sums = []
    for g in range(2):
        weights = d_r[:, g * GROUP : (g + 1) * GROUP, :].reshape(HALF_LANES, PIX)
        picked = code[:, g * HALF_LANES : (g + 1) * HALF_LANES]

        def one_band(j, value, g=g, weights=weights, picked=picked):
            every = dot(tiles[g * 4 + j], weights, NT)
            for t in range(8):
                value = value + jnp.where(
                    picked == j * 8 + t, every[t * DET : (t + 1) * DET, :], 0.0
                )
            return value

        sums.append(lax.fori_loop(0, 4, one_band, jnp.zeros((DET, HALF_LANES), F32)))
    value = jnp.concatenate(sums, axis=1)
    band = tab_ref[2:3, :]
    spread = jnp.concatenate(
        [
            jnp.where(band == j, value[h * HALF_DET : (h + 1) * HALF_DET, :], 0.0).astype(BF16)
            for h in range(NF)
            for j in range(NJ)
        ],
        axis=0,
    )
    together = dot(sel_s[...], spread, NT).astype(BF16)
    for h in range(NF):
        v_s[h] = together[:, h * 128 : (h + 1) * 128].reshape(NS, 16, 128)

    def v_copy(k, dst):
        other = lax.rem(me + k, NF * NS)
        oh, os = other // NS, lax.rem(other, NS)
        return pltpu.make_async_remote_copy(
            src_ref=v_s.at[oh, os], dst_ref=v_r.at[dst],
            send_sem=vs_sem.at[k], recv_sem=vr_sem.at[k],
            device_id=(oh, z, os), device_id_type=MESH,
        )

    def start_v(k, _):
        v_copy(k, me).start()
        return 0

    def wait_v(k, _):
        v_copy(k, lax.rem(me + NF * NS - k, NF * NS)).wait_recv()
        return 0

    lax.fori_loop(1, NF * NS, start_v, 0)
    v_r[me] = v_s[f, s]
    lax.fori_loop(1, NF * NS, wait_v, 0)

    found = dot(sel_v[...], v_r[...].reshape(NF * NS * 16, 128))
    fold = ((row & (HALF_DET - 1)) == lane).astype(BF16)
    lane_band = (lane // HALF_DET).astype(F32)
    for c in range(SD // 128):
        kept = jnp.where(
            lane_band == turned_cols[:, 16 + c : 17 + c], found[c * 128 : (c + 1) * 128, :], 0.0
        )
        out_ref[c * 128 : (c + 1) * 128, :] = dot(kept.astype(BF16), fold)[:, :HALF_DET].astype(BF16)

    exchange.wait_send()

    def sent(k, _):
        y_copy(k, s).wait_send()
        d_copy(k, s).wait_send()
        return 0

    def sent_v(k, _):
        v_copy(k, me).wait_send()
        return 0

    lax.fori_loop(1, NS, sent, 0)
    lax.fori_loop(1, NF * NS, sent_v, 0)
    for k in range(1, 9):
        for way in (0, 1) if k < 8 else (0,):
            ring(k, way).wait_send()


def band_matrix(band_index, band_weight, first_freq, freq_count):
    freq_ids = first_freq + lax.iota(I32, freq_count)
    matches = (band_index[:, :, None] == freq_ids[None, None, :]).astype(F32)
    return jnp.sum(matches * band_weight[:, :, None], axis=1).astype(BF16)


def on_device(alm, band_index, band_weight, legendre, orders, owner, tile_local, interp):
    freqs = alm.shape[0]
    band = band_matrix(band_index, band_weight, lax.axis_index("freq") * freqs, freqs)
    part = jnp.dot(band, alm.reshape(freqs, 2 * L), preferred_element_type=F32)
    order_rows = jnp.broadcast_to(orders[:, None], (orders.shape[0], 128))
    dma = pltpu.SemaphoreType.DMA
    vmem = pl.BlockSpec(memory_space=pltpu.VMEM)
    anywhere = pl.BlockSpec(memory_space=pl.ANY)
    return pl.pallas_call(
        kernel,
        out_shape=jax.ShapeDtypeStruct((SD, HALF_DET), BF16),
        in_specs=[
            pl.BlockSpec(memory_space=pltpu.SMEM), vmem, anywhere, anywhere, vmem, vmem, vmem, vmem,
        ],
        out_specs=vmem,
        scratch_shapes=[
            pltpu.VMEM((DET, 2 * L), BF16),
            pltpu.VMEM((DET, 2 * L), BF16),
            pltpu.VMEM((L, RH), BF16),
            pltpu.VMEM((SD, PIX), BF16),
            pltpu.VMEM((4 * ROWS, SD), BF16),
            pltpu.VMEM((NS, ROWS, PIX), BF16),
            pltpu.VMEM((NS, ROWS, PIX), BF16),
            pltpu.VMEM((NS, 32, 128), BF16),
            pltpu.VMEM((NS, 32, 128), BF16),
            pltpu.VMEM((NS * 16, 128), F32),
            pltpu.VMEM((NG * 32, 1024), BF16),
            pltpu.VMEM((NG * 32, NPHI), BF16),
            pltpu.VMEM((1024, NPHI), F32),
            pltpu.VMEM((NJ, 8 * DET, PIX), BF16),
            pltpu.VMEM((NF, NS, 16, 128), BF16),
            pltpu.VMEM((NF * NS, 16, 128), BF16),
            pltpu.VMEM((128, 128), F32),
            pltpu.VMEM((SD, NF * NS * 16), BF16),
            pltpu.VMEM((256, LANES), BF16),
            pltpu.VMEM((16, 128), I32),
            dma((2,)), dma((2,)), dma((NS,)), dma((NS,)), dma((NS,)), dma((NS,)),
            dma((NG,)), dma((NG,)), dma((NF * NS,)), dma((NF * NS,)),
        ],
        compiler_params=pltpu.CompilerParams(
            collective_id=0, has_side_effects=True, vmem_limit_bytes=48 * 2**20
        ),
    )(
        orders, part, legendre, interp, owner.reshape(16, 128), tile_local.reshape(16, 128),
        order_rows, jnp.asarray(lane_table()),
    )


def solution(mesh):
    placed = (
        P("freq", ("grp", "sub"), None, None),
        P(),
        P(),
        P(("grp", "sub"), None, None),
        P(),
        P(("grp", "sub"), None),
        P(("grp", "sub")),
        P(("grp", "sub"), None),
    )
    return jax.shard_map(
        on_device, mesh=mesh, in_specs=placed, out_specs=P(("grp", "sub"), "freq"), check_vma=False
    )
```

```python
import math

import jax
import jax.numpy as jnp
import numpy as np
from jax import lax
from jax.experimental import pallas as pl
from jax.experimental.pallas import tpu as pltpu
from jax.sharding import PartitionSpec as P

MESH = pl.DeviceIdType.MESH
F32, BF16, I32 = jnp.float32, jnp.bfloat16, jnp.int32
NF, NG, NS = 2, 16, 16
DET = 32
HALF_DET = DET // NF
L = 1024
RH = 512
NPHI = 1024
SD = 2048
PIX = 512
CAP = 12
NJ = 8
ROWS = NJ * CAP
GROUP = ROWS // 2
HALF_LANES = NS * GROUP
LANES = 2 * HALF_LANES
NN = (((1,), (0,)), ((), ()))
NT = (((1,), (1,)), ((), ()))
TN = (((0,), (0,)), ((), ()))


def dot(a, b, dims=NN):
    return lax.dot_general(a, b, dims, preferred_element_type=F32)


def lane_table():
    lane = np.arange(LANES)
    g, rest = lane // HALF_LANES, lane % HALF_LANES
    s, j4, k = rest // GROUP, rest % GROUP // CAP, rest % CAP
    table = np.zeros((8, LANES), np.int32)
    table[0] = s * NJ + g * 4 + j4
    table[1] = k
    table[2] = g * 4 + j4
    table[3] = s * 16 + k
    table[4] = j4 * 8
    return table


def kernel(
    alm_ref, bidx_hbm, bwt_hbm, leg_ref, ord_hbm, own_hbm, tile_hbm, int_ref, tab_hbm, out_ref,
    bidx_ref, bwt_ref, ord_ref, own_ref, tile_ref, tab_ref, ordb_ref,
    leg_v, int_v, pick, d_s, d_r, t_s, t_r, y_s, y_r, y_f, coef, basis, acc, tiles,
    v_s, v_r, cols, sel_v, sel_s, rank_v,
    loc_sem, ts_sem, tr_sem, ys_sem, yr_sem, ds_sem, dr_sem, rs_sem, rr_sem, vs_sem, vr_sem,
):
    f, z, s = lax.axis_index("freq"), lax.axis_index("grp"), lax.axis_index("sub")
    me = f * NS + s

    leg_copy = pltpu.make_async_copy(leg_ref.at[0], leg_v, loc_sem.at[0])
    int_copy = pltpu.make_async_copy(int_ref, int_v, loc_sem.at[1])
    small = [
        pltpu.make_async_copy(source, target, loc_sem.at[2 + n])
        for n, (source, target) in enumerate((
            (bidx_hbm, bidx_ref), (bwt_hbm, bwt_ref), (ord_hbm, ord_ref),
            (own_hbm, own_ref), (tile_hbm, tile_ref), (tab_hbm, tab_ref),
        ))
    ]
    for copy in small:
        copy.start()
    leg_copy.start()
    int_copy.start()

    barrier = pltpu.get_barrier_semaphore()

    def greet(k, _):
        other = lax.rem(me + k, NF * NS)
        pl.semaphore_signal(
            barrier, inc=1, device_id=(other // NS, z, lax.rem(other, NS)), device_id_type=MESH
        )
        return 0

    lax.fori_loop(1, NF * NS, greet, 0)
    for hops in (1, 2, NG - 2, NG - 1):
        pl.semaphore_signal(
            barrier, inc=1, device_id=(f, lax.rem(z + hops, NG), s), device_id_type=MESH
        )

    for copy in small:
        copy.wait()
    freqs = alm_ref.shape[0]
    freq = lax.broadcasted_iota(I32, (DET, freqs), 1) + f * freqs
    band = jnp.zeros((DET, freqs), F32)
    for k in range(bidx_ref.shape[1]):
        band = band + jnp.where(bidx_ref[:, k : k + 1] == freq, bwt_ref[:, k : k + 1], 0.0)
    part = dot(band.astype(BF16), alm_ref[...])
    for h in range(2):
        spread_rows = jnp.broadcast_to(ord_ref[h : h + 1, :].astype(F32), (128, 128))
        ordb_ref[h * 128 : (h + 1) * 128, :] = spread_rows.T.astype(I32)

    degree = lax.rem(lax.broadcasted_iota(I32, (DET, 2 * L), 1), L)
    order = ordb_ref[pl.ds(z * NS + s, 1), :][:, :1]
    part = jnp.where(degree >= order, part, 0.0).astype(BF16)
    leg_copy.wait()
    cyc = dot(jnp.concatenate([part[:, :L], part[:, L:]], axis=0), leg_v[...])
    turn = lax.broadcasted_iota(I32, (DET, RH), 1) & 3
    quads = (
        lax.broadcasted_iota(I32, (128, RH), 1) // 4 == lax.broadcasted_iota(I32, (128, RH), 0)
    ).astype(BF16)
    for h in range(NF):
        pair = []
        for c in range(2):
            one = cyc[c * DET : (c + 1) * DET, h * RH : (h + 1) * RH]
            spread = jnp.concatenate([jnp.where(turn == i, one, 0.0) for i in range(4)], axis=0)
            pair.append(dot(quads, spread.astype(BF16), NT).reshape(NS, NJ, 128))
        y_s[h] = jnp.concatenate(pair, axis=1).astype(BF16)

    def y_copy(k, dst):
        other = lax.rem(me + k, NF * NS)
        oh, os = other // NS, lax.rem(other, NS)
        return pltpu.make_async_remote_copy(
            src_ref=y_s.at[oh, os], dst_ref=y_r.at[dst],
            send_sem=ys_sem.at[k], recv_sem=yr_sem.at[k],
            device_id=(oh, z, os), device_id_type=MESH,
        )

    def start_y(k, _):
        y_copy(k, me).start()
        return 0

    pl.semaphore_wait(barrier, NF * NS - 1 + 4)
    lax.fori_loop(1, NF * NS, start_y, 0)
    y_r[me] = y_s[f, s]

    lane = lax.broadcasted_iota(I32, (128, 128), 1)
    row = lax.broadcasted_iota(I32, (128, 128), 0)
    before = (row < lane).astype(BF16)
    band_row = lax.broadcasted_iota(I32, (NF * NS * NJ, 128), 0)
    rank_row = lax.broadcasted_iota(I32, (16, 128), 0)
    seen = jnp.zeros((NF * NS * NJ, 1), F32)
    slot_tile = jnp.zeros((16, NF * NS * NJ), F32)
    for c in range(SD // 128):
        named = band_row == own_ref[c : c + 1, :]
        ones = jnp.where(named, 1.0, 0.0)
        marks = ones.astype(BF16)
        count = dot(marks, before) + seen
        rank = jnp.sum(jnp.where(named, count, 0.0), axis=0, keepdims=True)
        seen = seen + jnp.sum(ones, axis=1, keepdims=True)
        rank_i = rank.astype(I32)
        rank_v[c : c + 1, :] = rank_i
        ids = jnp.where(rank_row == rank_i, tile_ref[c : c + 1, :].astype(F32), 0.0)
        slot_tile = slot_tile + dot(ids.astype(BF16), marks, NT)
    half_tile = jnp.where(f == 0, slot_tile[:, :128], slot_tile[:, 128:])
    lane16 = lax.broadcasted_iota(I32, (16, 128), 1)
    mine16 = lane16 // NJ == s

    def put_tiles(other, _):
        turned = pltpu.roll(half_tile, lax.rem(s - other + NS, NS) * NJ, 1)
        t_s[other] = jnp.where(mine16, turned, 0.0).astype(BF16)
        return 0

    lax.fori_loop(0, NS, put_tiles, 0)

    int_copy.wait()
    slot_row = lax.broadcasted_iota(I32, (4 * ROWS, 128), 0)

    def pack(q, _):
        wanted = slot_row + q * (4 * ROWS)
        for c in range(SD // 128):
            key = (own_ref[c : c + 1, :] - f * 128) * CAP + rank_v[c : c + 1, :]
            pick[:, c * 128 : (c + 1) * 128] = jnp.where(wanted == key, 1.0, 0.0).astype(BF16)
        packed = dot(pick[...], int_v[...]).astype(BF16)
        for n in range(4):
            d_s[q * 4 + n] = packed[n * ROWS : (n + 1) * ROWS, :]
        return 0

    lax.fori_loop(0, 4, pack, 0)

    def t_copy(k, dst):
        return pltpu.make_async_remote_copy(
            src_ref=t_s.at[lax.rem(s + k, NS)], dst_ref=t_r.at[dst],
            send_sem=ts_sem.at[k], recv_sem=tr_sem.at[k],
            device_id=(f, z, lax.rem(s + k, NS)), device_id_type=MESH,
        )

    def d_copy(k, dst):
        return pltpu.make_async_remote_copy(
            src_ref=d_s.at[lax.rem(s + k, NS)], dst_ref=d_r.at[dst],
            send_sem=ds_sem.at[k], recv_sem=dr_sem.at[k],
            device_id=(f, z, lax.rem(s + k, NS)), device_id_type=MESH,
        )

    def start_d(k, _):
        t_copy(k, s).start()
        d_copy(k, s).start()
        return 0

    lax.fori_loop(1, NS, start_d, 0)
    t_r[s] = t_s[s]
    d_r[s] = d_s[s]

    def wait_y(k, _):
        y_copy(k, lax.rem(me + NF * NS - k, NF * NS)).wait_recv()
        return 0

    lax.fori_loop(1, NF * NS, wait_y, 0)
    y_f[...] = (y_r[0:NS].astype(F32) + y_r[NS : 2 * NS].astype(F32)).reshape(NS * 16, 128)
    for c in range(2):
        for j in range(NJ):
            coef[c * 16 : (c + 1) * 16, j * 128 : (j + 1) * 128] = y_f[
                pl.ds(c * NJ + j, NS, stride=16), :
            ].astype(BF16)

    def slot(d, way):
        return 0 if d == 0 else 2 * d - (way == 0)

    def ring(d, hops, way, c):
        source, target = slot(d, way) * 32 + c * 16, slot(d + hops, way) * 32 + c * 16
        sem = slot(d + hops, way) * 2 + c
        return pltpu.make_async_remote_copy(
            src_ref=coef.at[pl.ds(source, 16), :], dst_ref=coef.at[pl.ds(target, 16), :],
            send_sem=rs_sem.at[sem], recv_sem=rr_sem.at[sem],
            device_id=(f, lax.rem(z + (hops if way == 0 else NG - hops), NG), s), device_id_type=MESH,
        )

    def ring_step(d):
        for hops in (2, 1):
            for c in range(2):
                for way in range(2):
                    if d > 0 and hops == 2:
                        ring(d - 2, 2, way, c).wait_recv()
                    if d + hops < 8 or way == 0:
                        ring(d, hops, way, c).start()

    def ring_wait(*steps):
        for d, hops in steps:
            for c in range(2):
                for way in range(2):
                    if d + hops < 8 or way == 0:
                        ring(d, hops, way, c).wait_recv()

    def sky_first(j, _):
        at = pl.multiple_of(j * 128, 128)
        acc[pl.ds(at, 128), :] = dot(coef[0:256, pl.ds(at, 128)], basis[0:256, :], TN)
        return 0

    ring_step(0)

    def make_basis(p, _):
        hops = (p + 1) // 2
        zz = lax.rem(z + NG + (1 - 2 * lax.rem(p, 2)) * hops, NG)
        orders = ordb_ref[pl.ds(pl.multiple_of(zz * NS, NS), NS), :]
        lon = lax.broadcasted_iota(I32, (NS, 128), 1)
        fine = ((orders * lon) & (NPHI - 1)).astype(F32) * (2.0 * math.pi / NPHI)
        coarse = ((orders * (lon * 128)) & (NPHI - 1)).astype(F32) * (2.0 * math.pi / NPHI)
        weight = jnp.where(orders == 0, 1.0, 2.0)
        cos_u, sin_u = weight * jnp.cos(fine), weight * jnp.sin(fine)
        cos_t, sin_t = jnp.cos(coarse), jnp.sin(coarse)
        top = pl.multiple_of(p * 32, 32)
        for t in range(8):
            ct, st = cos_t[:, t : t + 1], sin_t[:, t : t + 1]
            basis[pl.ds(top, NS), t * 128 : (t + 1) * 128] = (ct * cos_u - st * sin_u).astype(BF16)
            basis[pl.ds(top + NS, NS), t * 128 : (t + 1) * 128] = (-(st * cos_u + ct * sin_u)).astype(BF16)
        return 0

    lax.fori_loop(0, NG, make_basis, 0)

    sel_s[...] = (lax.broadcasted_iota(I32, (256, LANES), 0) == tab_ref[3:4, :]).astype(BF16)
    cols[...] = jnp.zeros_like(cols)
    cols[0:16, :] = ((own_ref[...] // NJ) * 16 + rank_v[...]).astype(F32)
    cols[16:32, :] = (own_ref[...] & (NJ - 1)).astype(F32)
    turned_cols = cols[...].T
    place = lax.broadcasted_iota(I32, (128, NF * NS * 16), 1).astype(F32)
    for c in range(SD // 128):
        sel_v[c * 128 : (c + 1) * 128, :] = (place == turned_cols[:, c : c + 1]).astype(BF16)

    ring_step(2)
    ring_step(4)
    ring_wait((0, 1), (2, 1))
    lax.fori_loop(0, 4, sky_first, 0)
    ring_step(6)
    lax.fori_loop(4, 8, sky_first, 0)
    ring_wait((4, 1), (6, 2), (6, 1))

    def sky_last(j, _):
        at = pl.multiple_of(j * 128, 128)
        sky = acc[pl.ds(at, 128), :] + dot(coef[256:512, pl.ds(at, 128)], basis[256:512, :], TN)
        sky = sky.astype(BF16)
        for i in range(4):
            for t in range(8):
                tiles[j, t * DET : (t + 1) * DET, i * 128 : (i + 1) * 128] = sky[
                    i * DET : (i + 1) * DET, t * 128 : (t + 1) * 128
                ]
        return 0

    lax.fori_loop(0, NJ, sky_last, 0)

    def wait_t(k, _):
        t_copy(k, lax.rem(s + NS - k, NS)).wait_recv()
        return 0

    lax.fori_loop(1, NS, wait_t, 0)
    tile_sum = jnp.sum(t_r[...].astype(F32), axis=0).astype(BF16)
    here = (lax.broadcasted_iota(I32, (128, LANES), 0) == tab_ref[0:1, :]).astype(BF16)
    by_rank = dot(tile_sum, here)
    own_rank = lax.broadcasted_iota(I32, (16, LANES), 0) == tab_ref[1:2, :]
    code = jnp.sum(jnp.where(own_rank, by_rank, 0.0), axis=0, keepdims=True).astype(I32)
    code = code + tab_ref[4:5, :]

    def wait_d(k, _):
        d_copy(k, lax.rem(s + NS - k, NS)).wait_recv()
        return 0

    lax.fori_loop(1, NS, wait_d, 0)
    sums = []
    for g in range(2):
        weights = d_r[:, g * GROUP : (g + 1) * GROUP, :].reshape(HALF_LANES, PIX)
        picked = code[:, g * HALF_LANES : (g + 1) * HALF_LANES]

        def one_band(j, value, g=g, weights=weights, picked=picked):
            every = dot(tiles[g * 4 + j], weights, NT)
            for t in range(8):
                value = value + jnp.where(
                    picked == j * 8 + t, every[t * DET : (t + 1) * DET, :], 0.0
                )
            return value

        sums.append(lax.fori_loop(0, 4, one_band, jnp.zeros((DET, HALF_LANES), F32)))
    value = jnp.concatenate(sums, axis=1)
    band = tab_ref[2:3, :]
    spread = jnp.concatenate(
        [
            jnp.where(band == j, value[h * HALF_DET : (h + 1) * HALF_DET, :], 0.0).astype(BF16)
            for h in range(NF)
            for j in range(NJ)
        ],
        axis=0,
    )
    together = dot(sel_s[...], spread, NT).astype(BF16)
    for h in range(NF):
        v_s[h] = together[:, h * 128 : (h + 1) * 128].reshape(NS, 16, 128)

    def v_copy(k, dst):
        other = lax.rem(me + k, NF * NS)
        oh, os = other // NS, lax.rem(other, NS)
        return pltpu.make_async_remote_copy(
            src_ref=v_s.at[oh, os], dst_ref=v_r.at[dst],
            send_sem=vs_sem.at[k], recv_sem=vr_sem.at[k],
            device_id=(oh, z, os), device_id_type=MESH,
        )

    def start_v(k, _):
        v_copy(k, me).start()
        return 0

    def wait_v(k, _):
        v_copy(k, lax.rem(me + NF * NS - k, NF * NS)).wait_recv()
        return 0

    lax.fori_loop(1, NF * NS, start_v, 0)
    v_r[me] = v_s[f, s]
    lax.fori_loop(1, NF * NS, wait_v, 0)

    found = dot(sel_v[...], v_r[...].reshape(NF * NS * 16, 128))
    fold = (rank_row == (lane16 & (HALF_DET - 1))).astype(BF16)
    lane_band = (lane // HALF_DET).astype(F32)
    for c in range(SD // 128):
        kept = jnp.where(
            lane_band == turned_cols[:, 16 + c : 17 + c], found[c * 128 : (c + 1) * 128, :], 0.0
        )
        out_ref[:, c * 128 : (c + 1) * 128] = dot(fold, kept.astype(BF16), NT).astype(BF16)

    def sent(k, _):
        t_copy(k, s).wait_send()
        d_copy(k, s).wait_send()
        return 0

    def sent_all(k, _):
        y_copy(k, me).wait_send()
        v_copy(k, me).wait_send()
        return 0

    lax.fori_loop(1, NS, sent, 0)
    lax.fori_loop(1, NF * NS, sent_all, 0)
    for d in range(0, 8, 2):
        for hops in (1, 2):
            for c in range(2):
                for way in range(2):
                    if d + hops < 8 or way == 0:
                        ring(d, hops, way, c).wait_send()


def on_device(alm, band_index, band_weight, legendre, orders, owner, tile_local, interp):
    dma = pltpu.SemaphoreType.DMA
    vmem = pl.BlockSpec(memory_space=pltpu.VMEM)
    hbm = pl.BlockSpec(memory_space=pltpu.HBM)
    turned = pl.pallas_call(
        kernel,
        out_shape=jax.ShapeDtypeStruct((HALF_DET, SD), BF16),
        in_specs=[vmem] + [hbm] * 8,
        out_specs=vmem,
        scratch_shapes=[
            pltpu.VMEM(band_index.shape, I32),
            pltpu.VMEM(band_weight.shape, F32),
            pltpu.VMEM((2, 128), I32),
            pltpu.VMEM((16, 128), I32),
            pltpu.VMEM((16, 128), I32),
            pltpu.VMEM((8, LANES), I32),
            pltpu.VMEM((256, 128), I32),
            pltpu.VMEM(legendre.shape[1:], BF16),
            pltpu.VMEM((SD, PIX), BF16),
            pltpu.VMEM((4 * ROWS, SD), BF16),
            pltpu.VMEM((NS, ROWS, PIX), BF16),
            pltpu.VMEM((NS, ROWS, PIX), BF16),
            pltpu.VMEM((NS, 16, 128), BF16),
            pltpu.VMEM((NS, 16, 128), BF16),
            pltpu.VMEM((NF, NS, 16, 128), BF16),
            pltpu.VMEM((NF * NS, 16, 128), BF16),
            pltpu.VMEM((NS * 16, 128), F32),
            pltpu.VMEM((NG * 32, 1024), BF16),
            pltpu.VMEM((NG * 32, NPHI), BF16),
            pltpu.VMEM((1024, NPHI), F32),
            pltpu.VMEM((NJ, 8 * DET, PIX), BF16),
            pltpu.VMEM((NF, NS, 16, 128), BF16),
            pltpu.VMEM((NF * NS, 16, 128), BF16),
            pltpu.VMEM((128, 128), F32),
            pltpu.VMEM((SD, NF * NS * 16), BF16),
            pltpu.VMEM((256, LANES), BF16),
            pltpu.VMEM((16, 128), I32),
            dma((8,)), dma((NS,)), dma((NS,)), dma((NF * NS,)), dma((NF * NS,)), dma((NS,)), dma((NS,)),
            dma((2 * NG,)), dma((2 * NG,)), dma((NF * NS,)), dma((NF * NS,)),
        ],
        compiler_params=pltpu.CompilerParams(
            collective_id=0, has_side_effects=True, vmem_limit_bytes=65_500_000
        ),
    )(
        alm.reshape(alm.shape[0], 2 * L), band_index, band_weight, legendre, orders.reshape(2, 128),
        owner.reshape(16, 128), tile_local.reshape(16, 128), interp, jnp.asarray(lane_table()),
    )
    return turned.T


def solution(mesh):
    placed = (
        P("freq", ("grp", "sub"), None, None),
        P(),
        P(),
        P(("grp", "sub"), None, None),
        P(),
        P(("grp", "sub"), None),
        P(("grp", "sub")),
        P(("grp", "sub"), None),
    )
    return jax.shard_map(
        on_device, mesh=mesh, in_specs=placed, out_specs=P(("grp", "sub"), "freq"), check_vma=False
    )
```

```python
import math

import jax
import jax.numpy as jnp
import numpy as np
from jax import lax
from jax.experimental import pallas as pl
from jax.experimental.pallas import tpu as pltpu
from jax.sharding import PartitionSpec as P

MESH = pl.DeviceIdType.MESH
F32, BF16, I32 = jnp.float32, jnp.bfloat16, jnp.int32
NF, NG, NS = 2, 16, 16
DET = 32
HALF_DET = DET // NF
L = 1024
RH = 512
NPHI = 1024
SD = 2048
PIX = 512
CAP = 12
NJ = 8
ROWS = NJ * CAP
GROUP = ROWS // 2
HALF_LANES = NS * GROUP
LANES = 2 * HALF_LANES
NN = (((1,), (0,)), ((), ()))
NT = (((1,), (1,)), ((), ()))
TN = (((0,), (0,)), ((), ()))


def dot(a, b, dims=NN):
    return lax.dot_general(a, b, dims, preferred_element_type=F32)


def lane_table():
    lane = np.arange(LANES)
    g, rest = lane // HALF_LANES, lane % HALF_LANES
    s, j4, k = rest // GROUP, rest % GROUP // CAP, rest % CAP
    table = np.zeros((8, LANES), np.int32)
    table[0] = s * NJ + g * 4 + j4
    table[1] = k
    table[2] = g * 4 + j4
    table[3] = s * 16 + k
    table[4] = j4 * 8
    return table


def kernel(
    alm_hbm, bidx_hbm, bwt_hbm, leg_ref, ord_hbm, own_hbm, tile_hbm, int_ref, tab_hbm, out_ref,
    alm_ref, bidx_ref, bwt_ref, ord_ref, own_ref, tile_ref, tab_ref, ordb_ref,
    leg_v, int_v, pick, d_s, d_r, t_s, t_r, y_s, y_r, y_f, coef, coef_t, basis, acc, tiles,
    v_s, v_r, cols, sel_v, sel_s, rank_v,
    loc_sem, ts_sem, tr_sem, ys_sem, yr_sem, ds_sem, dr_sem, rs_sem, rr_sem, vs_sem, vr_sem,
):
    f, z, s = lax.axis_index("freq"), lax.axis_index("grp"), lax.axis_index("sub")
    me = f * NS + s

    leg_copy = pltpu.make_async_copy(leg_ref.at[0], leg_v, loc_sem.at[0])
    int_copy = pltpu.make_async_copy(int_ref, int_v, loc_sem.at[1])
    small = [
        pltpu.make_async_copy(source, target, loc_sem.at[2 + n])
        for n, (source, target) in enumerate((
            (alm_hbm, alm_ref), (bidx_hbm, bidx_ref), (bwt_hbm, bwt_ref), (ord_hbm, ord_ref),
            (own_hbm, own_ref), (tile_hbm, tile_ref), (tab_hbm, tab_ref),
        ))
    ]
    for copy in small:
        copy.start()
    leg_copy.start()
    int_copy.start()

    barrier = pltpu.get_barrier_semaphore()

    def greet(k, _):
        other = lax.rem(me + k, NF * NS)
        pl.semaphore_signal(
            barrier, inc=1, device_id=(other // NS, z, lax.rem(other, NS)), device_id_type=MESH
        )
        return 0

    lax.fori_loop(1, NF * NS, greet, 0)
    for hops in (1, 2, NG - 2, NG - 1):
        pl.semaphore_signal(
            barrier, inc=1, device_id=(f, lax.rem(z + hops, NG), s), device_id_type=MESH
        )

    for copy in small:
        copy.wait()
    freqs = alm_ref.shape[0]
    freq = lax.broadcasted_iota(I32, (DET, freqs), 1) + f * freqs
    band = jnp.zeros((DET, freqs), F32)
    for k in range(bidx_ref.shape[1]):
        band = band + jnp.where(bidx_ref[:, k : k + 1] == freq, bwt_ref[:, k : k + 1], 0.0)
    band = band.astype(BF16)
    part = jnp.concatenate([dot(band, alm_ref[:, c, :]) for c in range(2)], axis=1)
    for h in range(2):
        spread_rows = jnp.broadcast_to(ord_ref[h : h + 1, :].astype(F32), (128, 128))
        ordb_ref[h * 128 : (h + 1) * 128, :] = spread_rows.T.astype(I32)

    degree = lax.rem(lax.broadcasted_iota(I32, (DET, 2 * L), 1), L)
    order = ordb_ref[pl.ds(z * NS + s, 1), :][:, :1]
    part = jnp.where(degree >= order, part, 0.0).astype(BF16)
    leg_copy.wait()
    cyc = dot(jnp.concatenate([part[:, :L], part[:, L:]], axis=0), leg_v[...])
    turn = lax.broadcasted_iota(I32, (DET, RH), 1) & 3
    quads = (
        lax.broadcasted_iota(I32, (128, RH), 1) // 4 == lax.broadcasted_iota(I32, (128, RH), 0)
    ).astype(BF16)
    for h in range(NF):
        pair = []
        for c in range(2):
            one = cyc[c * DET : (c + 1) * DET, h * RH : (h + 1) * RH]
            spread = jnp.concatenate([jnp.where(turn == i, one, 0.0) for i in range(4)], axis=0)
            pair.append(dot(quads, spread.astype(BF16), NT).reshape(NS, NJ, 128))
        y_s[h] = jnp.concatenate(pair, axis=1).astype(BF16)

    def y_copy(k, dst):
        other = lax.rem(me + k, NF * NS)
        oh, os = other // NS, lax.rem(other, NS)
        return pltpu.make_async_remote_copy(
            src_ref=y_s.at[oh, os], dst_ref=y_r.at[dst],
            send_sem=ys_sem.at[k], recv_sem=yr_sem.at[k],
            device_id=(oh, z, os), device_id_type=MESH,
        )

    def start_y(k, _):
        y_copy(k, me).start()
        return 0

    pl.semaphore_wait(barrier, NF * NS - 1 + 4)
    lax.fori_loop(1, NF * NS, start_y, 0)
    y_r[me] = y_s[f, s]

    lane = lax.broadcasted_iota(I32, (128, 128), 1)
    row = lax.broadcasted_iota(I32, (128, 128), 0)
    before = (row < lane).astype(BF16)
    band_row = lax.broadcasted_iota(I32, (NF * NS * NJ, 128), 0)
    rank_row = lax.broadcasted_iota(I32, (16, 128), 0)
    seen = jnp.zeros((NF * NS * NJ, 1), F32)
    slot_tile = jnp.zeros((16, NF * NS * NJ), F32)
    for c in range(SD // 128):
        named = band_row == own_ref[c : c + 1, :]
        ones = jnp.where(named, 1.0, 0.0)
        marks = ones.astype(BF16)
        count = dot(marks, before) + seen
        rank = jnp.sum(jnp.where(named, count, 0.0), axis=0, keepdims=True)
        seen = seen + jnp.sum(ones, axis=1, keepdims=True)
        rank_i = rank.astype(I32)
        rank_v[c : c + 1, :] = rank_i
        ids = jnp.where(rank_row == rank_i, tile_ref[c : c + 1, :].astype(F32), 0.0)
        slot_tile = slot_tile + dot(ids.astype(BF16), marks, NT)
    half_tile = jnp.where(f == 0, slot_tile[:, :128], slot_tile[:, 128:])
    lane16 = lax.broadcasted_iota(I32, (16, 128), 1)
    mine16 = lane16 // NJ == s

    def put_tiles(other, _):
        turned = pltpu.roll(half_tile, lax.rem(s - other + NS, NS) * NJ, 1)
        t_s[other] = jnp.where(mine16, turned, 0.0).astype(BF16)
        return 0

    lax.fori_loop(0, NS, put_tiles, 0)

    int_copy.wait()
    slot_row = lax.broadcasted_iota(I32, (4 * ROWS, 128), 0)

    def pack(q, _):
        wanted = slot_row + q * (4 * ROWS)
        for c in range(SD // 128):
            key = (own_ref[c : c + 1, :] - f * 128) * CAP + rank_v[c : c + 1, :]
            pick[:, c * 128 : (c + 1) * 128] = jnp.where(wanted == key, 1.0, 0.0).astype(BF16)
        packed = dot(pick[...], int_v[...]).astype(BF16)
        for n in range(4):
            d_s[q * 4 + n] = packed[n * ROWS : (n + 1) * ROWS, :]
        return 0

    lax.fori_loop(0, 4, pack, 0)

    def t_copy(k, dst):
        return pltpu.make_async_remote_copy(
            src_ref=t_s.at[lax.rem(s + k, NS)], dst_ref=t_r.at[dst],
            send_sem=ts_sem.at[k], recv_sem=tr_sem.at[k],
            device_id=(f, z, lax.rem(s + k, NS)), device_id_type=MESH,
        )

    def d_copy(k, dst):
        return pltpu.make_async_remote_copy(
            src_ref=d_s.at[lax.rem(s + k, NS)], dst_ref=d_r.at[dst],
            send_sem=ds_sem.at[k], recv_sem=dr_sem.at[k],
            device_id=(f, z, lax.rem(s + k, NS)), device_id_type=MESH,
        )

    def start_d(k, _):
        t_copy(k, s).start()
        d_copy(k, s).start()
        return 0

    lax.fori_loop(1, NS, start_d, 0)
    t_r[s] = t_s[s]
    d_r[s] = d_s[s]

    def wait_y(k, _):
        y_copy(k, lax.rem(me + NF * NS - k, NF * NS)).wait_recv()
        return 0

    lax.fori_loop(1, NF * NS, wait_y, 0)
    y_f[...] = (y_r[0:NS].astype(F32) + y_r[NS : 2 * NS].astype(F32)).reshape(NS * 16, 128)
    for c in range(2):
        for j in range(NJ):
            coef[c * 16 : (c + 1) * 16, j * 128 : (j + 1) * 128] = y_f[
                pl.ds(c * NJ + j, NS, stride=16), :
            ].astype(BF16)

    def slot(d, way):
        return 0 if d == 0 else min(2 * d - (way == 0), NG - 1)

    def ring(d, hops, way, c):
        source, target = slot(d, way) * 32 + c * 16, slot(d + hops, way) * 32 + c * 16
        sem = slot(d + hops, way) * 2 + c
        return pltpu.make_async_remote_copy(
            src_ref=coef.at[pl.ds(source, 16), :], dst_ref=coef.at[pl.ds(target, 16), :],
            send_sem=rs_sem.at[sem], recv_sem=rr_sem.at[sem],
            device_id=(f, lax.rem(z + (hops if way == 0 else NG - hops), NG), s), device_id_type=MESH,
        )

    def ring_step(d):
        for hops in (2, 1):
            for c in range(2):
                for way in range(2):
                    if d > 0 and hops == 2:
                        ring(d - 2, 2, way, c).wait_recv()
                    if d + hops < 8 or way == c:
                        ring(d, hops, way, c).start()

    def ring_wait(*steps):
        for d, hops in steps:
            for c in range(2):
                for way in range(2):
                    if d + hops < 8 or way == c:
                        ring(d, hops, way, c).wait_recv()

    def sky_first(n, _):
        at = pl.ds(pl.multiple_of(n * 256, 256), 256)
        acc[:, at] = dot(coef_t[...], basis[0:256, at])
        return 0

    ring_step(0)

    def make_basis(p, _):
        hops = (p + 1) // 2
        zz = lax.rem(z + NG + (1 - 2 * lax.rem(p, 2)) * hops, NG)
        orders = ordb_ref[pl.ds(pl.multiple_of(zz * NS, NS), NS), :]
        lon = lax.broadcasted_iota(I32, (NS, 128), 1)
        fine = ((orders * lon) & (NPHI - 1)).astype(F32) * (2.0 * math.pi / NPHI)
        coarse = ((orders * (lon * 128)) & (NPHI - 1)).astype(F32) * (2.0 * math.pi / NPHI)
        weight = jnp.where(orders == 0, 1.0, 2.0)
        cos_u, sin_u = weight * jnp.cos(fine), weight * jnp.sin(fine)
        cos_t, sin_t = jnp.cos(coarse), jnp.sin(coarse)
        top = pl.multiple_of(p * 32, 32)
        for t in range(8):
            ct, st = cos_t[:, t : t + 1], sin_t[:, t : t + 1]
            basis[pl.ds(top, NS), t * 128 : (t + 1) * 128] = (ct * cos_u - st * sin_u).astype(BF16)
            basis[pl.ds(top + NS, NS), t * 128 : (t + 1) * 128] = (-(st * cos_u + ct * sin_u)).astype(BF16)
        return 0

    lax.fori_loop(0, NG, make_basis, 0)

    sel_s[...] = (lax.broadcasted_iota(I32, (256, LANES), 0) == tab_ref[3:4, :]).astype(BF16)
    cols[...] = jnp.zeros_like(cols)
    cols[0:16, :] = ((own_ref[...] // NJ) * 16 + rank_v[...]).astype(F32)
    cols[16:32, :] = (own_ref[...] & (NJ - 1)).astype(F32)
    turned_cols = cols[...].T
    place = lax.broadcasted_iota(I32, (128, NF * NS * 16), 1).astype(F32)
    for c in range(SD // 128):
        sel_v[c * 128 : (c + 1) * 128, :] = (place == turned_cols[:, c : c + 1]).astype(BF16)

    ring_step(2)
    ring_step(4)
    ring_wait((0, 1), (2, 1))
    coef_t[...] = coef[0:256, :].T
    lax.fori_loop(0, 2, sky_first, 0)
    ring_step(6)
    lax.fori_loop(2, 4, sky_first, 0)
    ring_wait((4, 1), (6, 2), (6, 1))

    def sky_last(n, _):
        at = pl.ds(pl.multiple_of(n * 256, 256), 256)
        sky = (acc[:, at] + dot(coef_t[...], basis[256:512, at])).astype(BF16)
        for h in range(2):
            to = pl.ds(pl.multiple_of((2 * n + h) * DET, DET), DET)
            for j in range(NJ):
                for i in range(4):
                    top = j * 128 + i * DET
                    tiles[j, to, i * 128 : (i + 1) * 128] = sky[
                        top : top + DET, h * 128 : (h + 1) * 128
                    ]
        return 0

    coef_t[...] = coef[256:512, :].T
    lax.fori_loop(0, 4, sky_last, 0)

    def wait_t(k, _):
        t_copy(k, lax.rem(s + NS - k, NS)).wait_recv()
        return 0

    lax.fori_loop(1, NS, wait_t, 0)
    tile_sum = jnp.sum(t_r[...].astype(F32), axis=0).astype(BF16)
    here = (lax.broadcasted_iota(I32, (128, LANES), 0) == tab_ref[0:1, :]).astype(BF16)
    by_rank = dot(tile_sum, here)
    own_rank = lax.broadcasted_iota(I32, (16, LANES), 0) == tab_ref[1:2, :]
    code = jnp.sum(jnp.where(own_rank, by_rank, 0.0), axis=0, keepdims=True).astype(I32)
    code = code + tab_ref[4:5, :]

    def wait_d(k, _):
        d_copy(k, lax.rem(s + NS - k, NS)).wait_recv()
        return 0

    lax.fori_loop(1, NS, wait_d, 0)
    sums = []
    for g in range(2):
        weights = d_r[:, g * GROUP : (g + 1) * GROUP, :].reshape(HALF_LANES, PIX)
        pixels = tiles[g * 4 : (g + 1) * 4].reshape(4 * 8 * DET, PIX)
        for n in range(HALF_LANES // 256):
            every = dot(pixels, weights[n * 256 : (n + 1) * 256, :], NT)
            picked = code[:, g * HALF_LANES + n * 256 : g * HALF_LANES + (n + 1) * 256]
            value = jnp.zeros((DET, 256), F32)
            for t in range(32):
                value = value + jnp.where(picked == t, every[t * DET : (t + 1) * DET, :], 0.0)
            sums.append(value)
    value = jnp.concatenate(sums, axis=1)
    band = tab_ref[2:3, :]
    spread = jnp.concatenate(
        [
            jnp.where(band == j, value[h * HALF_DET : (h + 1) * HALF_DET, :], 0.0).astype(BF16)
            for h in range(NF)
            for j in range(NJ)
        ],
        axis=0,
    )
    together = dot(sel_s[...], spread, NT).astype(BF16)
    for h in range(NF):
        v_s[h] = together[:, h * 128 : (h + 1) * 128].reshape(NS, 16, 128)

    def v_copy(k, dst):
        other = lax.rem(me + k, NF * NS)
        oh, os = other // NS, lax.rem(other, NS)
        return pltpu.make_async_remote_copy(
            src_ref=v_s.at[oh, os], dst_ref=v_r.at[dst],
            send_sem=vs_sem.at[k], recv_sem=vr_sem.at[k],
            device_id=(oh, z, os), device_id_type=MESH,
        )

    def start_v(k, _):
        v_copy(k, me).start()
        return 0

    def wait_v(k, _):
        v_copy(k, lax.rem(me + NF * NS - k, NF * NS)).wait_recv()
        return 0

    lax.fori_loop(1, NF * NS, start_v, 0)
    v_r[me] = v_s[f, s]
    lax.fori_loop(1, NF * NS, wait_v, 0)

    found = dot(sel_v[...], v_r[...].reshape(NF * NS * 16, 128))
    fold = (rank_row == (lane16 & (HALF_DET - 1))).astype(BF16)
    lane_band = (lane // HALF_DET).astype(F32)
    for c in range(SD // 128):
        kept = jnp.where(
            lane_band == turned_cols[:, 16 + c : 17 + c], found[c * 128 : (c + 1) * 128, :], 0.0
        )
        out_ref[:, c * 128 : (c + 1) * 128] = dot(fold, kept.astype(BF16), NT).astype(BF16)

    def sent(k, _):
        t_copy(k, s).wait_send()
        d_copy(k, s).wait_send()
        return 0

    def sent_all(k, _):
        y_copy(k, me).wait_send()
        v_copy(k, me).wait_send()
        return 0

    lax.fori_loop(1, NS, sent, 0)
    lax.fori_loop(1, NF * NS, sent_all, 0)
    for d in range(0, 8, 2):
        for hops in (1, 2):
            for c in range(2):
                for way in range(2):
                    if d + hops < 8 or way == c:
                        ring(d, hops, way, c).wait_send()


def on_device(alm, band_index, band_weight, legendre, orders, owner, tile_local, interp):
    dma = pltpu.SemaphoreType.DMA
    vmem = pl.BlockSpec(memory_space=pltpu.VMEM)
    hbm = pl.BlockSpec(memory_space=pltpu.HBM)
    turned = pl.pallas_call(
        kernel,
        out_shape=jax.ShapeDtypeStruct((HALF_DET, SD), BF16),
        in_specs=[hbm] * 9,
        out_specs=vmem,
        scratch_shapes=[
            pltpu.VMEM((alm.shape[0], 2, L), BF16),
            pltpu.VMEM(band_index.shape, I32),
            pltpu.VMEM(band_weight.shape, F32),
            pltpu.VMEM((2, 128), I32),
            pltpu.VMEM((16, 128), I32),
            pltpu.VMEM((16, 128), I32),
            pltpu.VMEM((8, LANES), I32),
            pltpu.VMEM((256, 128), I32),
            pltpu.VMEM(legendre.shape[1:], BF16),
            pltpu.VMEM((SD, PIX), BF16),
            pltpu.VMEM((4 * ROWS, SD), BF16),
            pltpu.VMEM((NS, ROWS, PIX), BF16),
            pltpu.VMEM((NS, ROWS, PIX), BF16),
            pltpu.VMEM((NS, 16, 128), BF16),
            pltpu.VMEM((NS, 16, 128), BF16),
            pltpu.VMEM((NF, NS, 16, 128), BF16),
            pltpu.VMEM((NF * NS, 16, 128), BF16),
            pltpu.VMEM((NS * 16, 128), F32),
            pltpu.VMEM((NG * 32, 1024), BF16),
            pltpu.VMEM((1024, 256), BF16),
            pltpu.VMEM((NG * 32, NPHI), BF16),
            pltpu.VMEM((1024, NPHI), F32),
            pltpu.VMEM((NJ, 8 * DET, PIX), BF16),
            pltpu.VMEM((NF, NS, 16, 128), BF16),
            pltpu.VMEM((NF * NS, 16, 128), BF16),
            pltpu.VMEM((128, 128), F32),
            pltpu.VMEM((SD, NF * NS * 16), BF16),
            pltpu.VMEM((256, LANES), BF16),
            pltpu.VMEM((16, 128), I32),
            dma((9,)), dma((NS,)), dma((NS,)), dma((NF * NS,)), dma((NF * NS,)), dma((NS,)), dma((NS,)),
            dma((2 * NG,)), dma((2 * NG,)), dma((NF * NS,)), dma((NF * NS,)),
        ],
        compiler_params=pltpu.CompilerParams(
            collective_id=0, has_side_effects=True, vmem_limit_bytes=65_500_000
        ),
    )(
        alm.reshape(alm.shape[0], 2, L), band_index, band_weight, legendre, orders.reshape(2, 128),
        owner.reshape(16, 128), tile_local.reshape(16, 128), interp, jnp.asarray(lane_table()),
    )
    return turned.T


def solution(mesh):
    placed = (
        P("freq", ("grp", "sub"), None, None),
        P(),
        P(),
        P(("grp", "sub"), None, None),
        P(),
        P(("grp", "sub"), None),
        P(("grp", "sub")),
        P(("grp", "sub"), None),
    )
    return jax.shard_map(
        on_device, mesh=mesh, in_specs=placed, out_specs=P(("grp", "sub"), "freq"), check_vma=False
    )
```

```python
import math

import jax
import jax.numpy as jnp
import numpy as np
from jax import lax
from jax.experimental import pallas as pl
from jax.experimental.pallas import tpu as pltpu
from jax.sharding import PartitionSpec as P

MESH = pl.DeviceIdType.MESH
F32, BF16, I32 = jnp.float32, jnp.bfloat16, jnp.int32
NF, NG, NS = 2, 16, 16
DET = 32
HALF_DET = DET // NF
L = 1024
RH = 512
NPHI = 1024
SD = 2048
PIX = 512
CAP = 12
NJ = 8
ROWS = NJ * CAP
GROUP = ROWS // 2
HALF_LANES = NS * GROUP
LANES = 2 * HALF_LANES
NN = (((1,), (0,)), ((), ()))
NT = (((1,), (1,)), ((), ()))
TN = (((0,), (0,)), ((), ()))


def dot(a, b, dims=NN):
    return lax.dot_general(a, b, dims, preferred_element_type=F32)


def lane_table():
    lane = np.arange(LANES)
    g, rest = lane // HALF_LANES, lane % HALF_LANES
    s, j4, k = rest // GROUP, rest % GROUP // CAP, rest % CAP
    table = np.zeros((8, LANES), np.int32)
    table[0] = s * NJ + g * 4 + j4
    table[1] = k
    table[2] = g * 4 + j4
    table[3] = s * 16 + k
    table[4] = j4 * 8
    return table


def kernel(
    alm_hbm, bidx_hbm, bwt_hbm, leg_ref, ord_hbm, own_hbm, tile_hbm, int_ref, tab_hbm, out_ref,
    alm_ref, bidx_ref, bwt_ref, ord_ref, own_ref, tile_ref, tab_ref, ordb_ref,
    leg_v, int_v, pick, d_s, d_r, t_s, t_r, y_s, y_r, y_f, coef, coef_t, basis, acc, tiles,
    v_s, v_r, cols, sel_v, sel_s, rank_v,
    loc_sem, ts_sem, tr_sem, ys_sem, yr_sem, ds_sem, dr_sem, rs_sem, rr_sem, vs_sem, vr_sem,
):
    f, z, s = lax.axis_index("freq"), lax.axis_index("grp"), lax.axis_index("sub")
    me = f * NS + s

    leg_copy = pltpu.make_async_copy(leg_ref.at[0], leg_v, loc_sem.at[0])
    int_copy = pltpu.make_async_copy(int_ref, int_v, loc_sem.at[1])
    small = [
        pltpu.make_async_copy(source, target, loc_sem.at[2 + n])
        for n, (source, target) in enumerate((
            (alm_hbm, alm_ref), (bidx_hbm, bidx_ref), (bwt_hbm, bwt_ref), (ord_hbm, ord_ref),
            (own_hbm, own_ref), (tile_hbm, tile_ref), (tab_hbm, tab_ref),
        ))
    ]
    for copy in small:
        copy.start()
    leg_copy.start()
    int_copy.start()

    barrier = pltpu.get_barrier_semaphore()

    def greet(k, _):
        other = lax.rem(me + k, NF * NS)
        pl.semaphore_signal(
            barrier, inc=1, device_id=(other // NS, z, lax.rem(other, NS)), device_id_type=MESH
        )
        return 0

    lax.fori_loop(1, NF * NS, greet, 0)
    for hops in (1, 2, NG - 2, NG - 1):
        pl.semaphore_signal(
            barrier, inc=1, device_id=(f, lax.rem(z + hops, NG), s), device_id_type=MESH
        )

    for copy in small:
        copy.wait()
    freqs = alm_ref.shape[0]
    freq = lax.broadcasted_iota(I32, (DET, freqs), 1) + f * freqs
    band = jnp.zeros((DET, freqs), F32)
    for k in range(bidx_ref.shape[1]):
        band = band + jnp.where(bidx_ref[:, k : k + 1] == freq, bwt_ref[:, k : k + 1], 0.0)
    band = band.astype(BF16)
    part = jnp.concatenate([dot(band, alm_ref[:, c, :]) for c in range(2)], axis=1)
    for h in range(2):
        spread_rows = jnp.broadcast_to(ord_ref[h : h + 1, :].astype(F32), (128, 128))
        ordb_ref[h * 128 : (h + 1) * 128, :] = spread_rows.T.astype(I32)

    degree = lax.rem(lax.broadcasted_iota(I32, (DET, 2 * L), 1), L)
    order = ordb_ref[pl.ds(z * NS + s, 1), :][:, :1]
    part = jnp.where(degree >= order, part, 0.0).astype(BF16)
    leg_copy.wait()
    cyc = dot(jnp.concatenate([part[:, :L], part[:, L:]], axis=0), leg_v[...])
    turn = lax.broadcasted_iota(I32, (DET, RH), 1) & 3
    quads = (
        lax.broadcasted_iota(I32, (128, RH), 1) // 4 == lax.broadcasted_iota(I32, (128, RH), 0)
    ).astype(BF16)
    for h in range(NF):
        pair = []
        for c in range(2):
            one = cyc[c * DET : (c + 1) * DET, h * RH : (h + 1) * RH]
            spread = jnp.concatenate([jnp.where(turn == i, one, 0.0) for i in range(4)], axis=0)
            pair.append(dot(quads, spread.astype(BF16), NT).reshape(NS, NJ, 128))
        y_s[h] = jnp.concatenate(pair, axis=1).astype(BF16)

    def y_copy(k, dst):
        other = lax.rem(me + k, NF * NS)
        oh, os = other // NS, lax.rem(other, NS)
        return pltpu.make_async_remote_copy(
            src_ref=y_s.at[oh, os], dst_ref=y_r.at[dst],
            send_sem=ys_sem.at[k], recv_sem=yr_sem.at[k],
            device_id=(oh, z, os), device_id_type=MESH,
        )

    def start_y(k, _):
        y_copy(k, me).start()
        return 0

    pl.semaphore_wait(barrier, NF * NS - 1 + 4)
    lax.fori_loop(1, NF * NS, start_y, 0)
    y_r[me] = y_s[f, s]

    lane = lax.broadcasted_iota(I32, (128, 128), 1)
    row = lax.broadcasted_iota(I32, (128, 128), 0)
    before = (row < lane).astype(BF16)
    band_row = lax.broadcasted_iota(I32, (NF * NS * NJ, 128), 0)
    rank_row = lax.broadcasted_iota(I32, (16, 128), 0)
    seen = jnp.zeros((NF * NS * NJ, 1), F32)
    slot_tile = jnp.zeros((16, NF * NS * NJ), F32)
    for c in range(SD // 128):
        named = band_row == own_ref[c : c + 1, :]
        ones = jnp.where(named, 1.0, 0.0)
        marks = ones.astype(BF16)
        count = dot(marks, before) + seen
        rank = jnp.sum(jnp.where(named, count, 0.0), axis=0, keepdims=True)
        seen = seen + jnp.sum(ones, axis=1, keepdims=True)
        rank_i = rank.astype(I32)
        rank_v[c : c + 1, :] = rank_i
        ids = jnp.where(rank_row == rank_i, tile_ref[c : c + 1, :].astype(F32), 0.0)
        slot_tile = slot_tile + dot(ids.astype(BF16), marks, NT)
    half_tile = jnp.where(f == 0, slot_tile[:, :128], slot_tile[:, 128:])
    lane16 = lax.broadcasted_iota(I32, (16, 128), 1)
    mine16 = lane16 // NJ == s

    def put_tiles(other, _):
        turned = pltpu.roll(half_tile, lax.rem(s - other + NS, NS) * NJ, 1)
        t_s[other] = jnp.where(mine16, turned, 0.0).astype(BF16)
        return 0

    lax.fori_loop(0, NS, put_tiles, 0)

    def t_copy(k, dst):
        return pltpu.make_async_remote_copy(
            src_ref=t_s.at[lax.rem(s + k, NS)], dst_ref=t_r.at[dst],
            send_sem=ts_sem.at[k], recv_sem=tr_sem.at[k],
            device_id=(f, z, lax.rem(s + k, NS)), device_id_type=MESH,
        )

    def d_copy(k, dst):
        return pltpu.make_async_remote_copy(
            src_ref=d_s.at[lax.rem(s + k, NS)], dst_ref=d_r.at[dst],
            send_sem=ds_sem.at[k], recv_sem=dr_sem.at[k],
            device_id=(f, z, lax.rem(s + k, NS)), device_id_type=MESH,
        )

    int_copy.wait()
    slot_row = lax.broadcasted_iota(I32, (ROWS, 128), 0)

    def pack(q, _):
        wanted = jnp.concatenate(
            [slot_row + lax.rem(s + q * 4 + n, NS) * ROWS for n in range(4)], axis=0
        )
        for c in range(SD // 128):
            key = (own_ref[c : c + 1, :] - f * 128) * CAP + rank_v[c : c + 1, :]
            pick[:, c * 128 : (c + 1) * 128] = jnp.where(wanted == key, 1.0, 0.0).astype(BF16)
        packed = dot(pick[...], int_v[...]).astype(BF16)
        for n in range(4):
            k = q * 4 + n
            d_s[lax.rem(s + k, NS)] = packed[n * ROWS : (n + 1) * ROWS, :]

            @pl.when(k > 0)
            def _(k=k):
                t_copy(k, s).start()
                d_copy(k, s).start()

        return 0

    lax.fori_loop(0, 2, pack, 0)
    t_r[s] = t_s[s]
    d_r[s] = d_s[s]

    def wait_y(k, _):
        y_copy(k, lax.rem(me + NF * NS - k, NF * NS)).wait_recv()
        return 0

    lax.fori_loop(1, NF * NS, wait_y, 0)
    y_f[...] = (y_r[0:NS].astype(F32) + y_r[NS : 2 * NS].astype(F32)).reshape(NS * 16, 128)
    for c in range(2):
        for j in range(NJ):
            coef[c * 16 : (c + 1) * 16, j * 128 : (j + 1) * 128] = y_f[
                pl.ds(c * NJ + j, NS, stride=16), :
            ].astype(BF16)

    def slot(d, way):
        return 0 if d == 0 else min(2 * d - (way == 0), NG - 1)

    def ring(d, hops, way, c):
        source, target = slot(d, way) * 32 + c * 16, slot(d + hops, way) * 32 + c * 16
        sem = slot(d + hops, way) * 2 + c
        return pltpu.make_async_remote_copy(
            src_ref=coef.at[pl.ds(source, 16), :], dst_ref=coef.at[pl.ds(target, 16), :],
            send_sem=rs_sem.at[sem], recv_sem=rr_sem.at[sem],
            device_id=(f, lax.rem(z + (hops if way == 0 else NG - hops), NG), s), device_id_type=MESH,
        )

    def ring_step(d):
        for hops in (2, 1):
            for c in range(2):
                for way in range(2):
                    if d > 0 and hops == 2:
                        ring(d - 2, 2, way, c).wait_recv()
                    if d + hops < 8 or way == c:
                        ring(d, hops, way, c).start()

    def ring_wait(*steps):
        for d, hops in steps:
            for c in range(2):
                for way in range(2):
                    if d + hops < 8 or way == c:
                        ring(d, hops, way, c).wait_recv()

    def sky_first(n, _):
        at = pl.ds(pl.multiple_of(n * 256, 256), 256)
        acc[:, at] = dot(coef_t[...], basis[0:256, at])
        return 0

    ring_step(0)
    lax.fori_loop(2, 4, pack, 0)

    def make_basis(p, _):
        hops = (p + 1) // 2
        zz = lax.rem(z + NG + (1 - 2 * lax.rem(p, 2)) * hops, NG)
        orders = ordb_ref[pl.ds(pl.multiple_of(zz * NS, NS), NS), :]
        lon = lax.broadcasted_iota(I32, (NS, 128), 1)
        fine = ((orders * lon) & (NPHI - 1)).astype(F32) * (2.0 * math.pi / NPHI)
        coarse = ((orders * (lon * 128)) & (NPHI - 1)).astype(F32) * (2.0 * math.pi / NPHI)
        weight = jnp.where(orders == 0, 1.0, 2.0)
        cos_u, sin_u = weight * jnp.cos(fine), weight * jnp.sin(fine)
        cos_t, sin_t = jnp.cos(coarse), jnp.sin(coarse)
        top = pl.multiple_of(p * 32, 32)
        for t in range(8):
            ct, st = cos_t[:, t : t + 1], sin_t[:, t : t + 1]
            basis[pl.ds(top, NS), t * 128 : (t + 1) * 128] = (ct * cos_u - st * sin_u).astype(BF16)
            basis[pl.ds(top + NS, NS), t * 128 : (t + 1) * 128] = (-(st * cos_u + ct * sin_u)).astype(BF16)
        return 0

    lax.fori_loop(0, NG, make_basis, 0)

    sel_s[...] = (lax.broadcasted_iota(I32, (256, LANES), 0) == tab_ref[3:4, :]).astype(BF16)
    cols[...] = jnp.zeros_like(cols)
    cols[0:16, :] = ((own_ref[...] // NJ) * 16 + rank_v[...]).astype(F32)
    cols[16:32, :] = (own_ref[...] & (NJ - 1)).astype(F32)
    turned_cols = cols[...].T
    place = lax.broadcasted_iota(I32, (128, NF * NS * 16), 1).astype(F32)
    for c in range(SD // 128):
        sel_v[c * 128 : (c + 1) * 128, :] = (place == turned_cols[:, c : c + 1]).astype(BF16)

    ring_step(2)
    ring_step(4)
    ring_wait((0, 1), (2, 1))
    coef_t[...] = coef[0:256, :].T
    lax.fori_loop(0, 2, sky_first, 0)
    ring_step(6)
    lax.fori_loop(2, 4, sky_first, 0)
    ring_wait((4, 1), (6, 2), (6, 1))

    def sky_last(n, _):
        at = pl.ds(pl.multiple_of(n * 256, 256), 256)
        sky = (acc[:, at] + dot(coef_t[...], basis[256:512, at])).astype(BF16)
        for h in range(2):
            to = pl.ds(pl.multiple_of((2 * n + h) * DET, DET), DET)
            for j in range(NJ):
                for i in range(4):
                    top = j * 128 + i * DET
                    tiles[j, to, i * 128 : (i + 1) * 128] = sky[
                        top : top + DET, h * 128 : (h + 1) * 128
                    ]
        return 0

    coef_t[...] = coef[256:512, :].T
    lax.fori_loop(0, 4, sky_last, 0)

    def wait_t(k, _):
        t_copy(k, lax.rem(s + NS - k, NS)).wait_recv()
        return 0

    lax.fori_loop(1, NS, wait_t, 0)
    tile_sum = jnp.sum(t_r[...].astype(F32), axis=0).astype(BF16)
    here = (lax.broadcasted_iota(I32, (128, LANES), 0) == tab_ref[0:1, :]).astype(BF16)
    by_rank = dot(tile_sum, here)
    own_rank = lax.broadcasted_iota(I32, (16, LANES), 0) == tab_ref[1:2, :]
    code = jnp.sum(jnp.where(own_rank, by_rank, 0.0), axis=0, keepdims=True).astype(I32)
    code = code + tab_ref[4:5, :]

    def wait_d(k, _):
        d_copy(k, lax.rem(s + NS - k, NS)).wait_recv()
        return 0

    lax.fori_loop(1, NS, wait_d, 0)
    sums = []
    for g in range(2):
        weights = d_r[:, g * GROUP : (g + 1) * GROUP, :].reshape(HALF_LANES, PIX)
        pixels = tiles[g * 4 : (g + 1) * 4].reshape(4 * 8 * DET, PIX)
        for n in range(HALF_LANES // 256):
            every = dot(pixels, weights[n * 256 : (n + 1) * 256, :], NT)
            picked = code[:, g * HALF_LANES + n * 256 : g * HALF_LANES + (n + 1) * 256]
            value = jnp.zeros((DET, 256), F32)
            for t in range(32):
                value = value + jnp.where(picked == t, every[t * DET : (t + 1) * DET, :], 0.0)
            sums.append(value)
    value = jnp.concatenate(sums, axis=1)
    band = tab_ref[2:3, :]
    spread = jnp.concatenate(
        [
            jnp.where(band == j, value[h * HALF_DET : (h + 1) * HALF_DET, :], 0.0).astype(BF16)
            for h in range(NF)
            for j in range(NJ)
        ],
        axis=0,
    )
    together = dot(sel_s[...], spread, NT).astype(BF16)
    for h in range(NF):
        v_s[h] = together[:, h * 128 : (h + 1) * 128].reshape(NS, 16, 128)

    def v_copy(k, dst):
        other = lax.rem(me + k, NF * NS)
        oh, os = other // NS, lax.rem(other, NS)
        return pltpu.make_async_remote_copy(
            src_ref=v_s.at[oh, os], dst_ref=v_r.at[dst],
            send_sem=vs_sem.at[k], recv_sem=vr_sem.at[k],
            device_id=(oh, z, os), device_id_type=MESH,
        )

    def start_v(k, _):
        v_copy(k, me).start()
        return 0

    def wait_v(k, _):
        v_copy(k, lax.rem(me + NF * NS - k, NF * NS)).wait_recv()
        return 0

    lax.fori_loop(1, NF * NS, start_v, 0)
    v_r[me] = v_s[f, s]
    lax.fori_loop(1, NF * NS, wait_v, 0)

    found = dot(sel_v[...], v_r[...].reshape(NF * NS * 16, 128))
    fold = (rank_row == (lane16 & (HALF_DET - 1))).astype(BF16)
    lane_band = (lane // HALF_DET).astype(F32)
    for c in range(SD // 128):
        kept = jnp.where(
            lane_band == turned_cols[:, 16 + c : 17 + c], found[c * 128 : (c + 1) * 128, :], 0.0
        )
        out_ref[:, c * 128 : (c + 1) * 128] = dot(fold, kept.astype(BF16), NT).astype(BF16)

    def sent(k, _):
        t_copy(k, s).wait_send()
        d_copy(k, s).wait_send()
        return 0

    def sent_all(k, _):
        y_copy(k, me).wait_send()
        v_copy(k, me).wait_send()
        return 0

    lax.fori_loop(1, NS, sent, 0)
    lax.fori_loop(1, NF * NS, sent_all, 0)
    for d in range(0, 8, 2):
        for hops in (1, 2):
            for c in range(2):
                for way in range(2):
                    if d + hops < 8 or way == c:
                        ring(d, hops, way, c).wait_send()


def on_device(alm, band_index, band_weight, legendre, orders, owner, tile_local, interp):
    dma = pltpu.SemaphoreType.DMA
    vmem = pl.BlockSpec(memory_space=pltpu.VMEM)
    hbm = pl.BlockSpec(memory_space=pltpu.HBM)
    turned = pl.pallas_call(
        kernel,
        out_shape=jax.ShapeDtypeStruct((HALF_DET, SD), BF16),
        in_specs=[hbm] * 9,
        out_specs=vmem,
        scratch_shapes=[
            pltpu.VMEM((alm.shape[0], 2, L), BF16),
            pltpu.VMEM(band_index.shape, I32),
            pltpu.VMEM(band_weight.shape, F32),
            pltpu.VMEM((2, 128), I32),
            pltpu.VMEM((16, 128), I32),
            pltpu.VMEM((16, 128), I32),
            pltpu.VMEM((8, LANES), I32),
            pltpu.VMEM((256, 128), I32),
            pltpu.VMEM(legendre.shape[1:], BF16),
            pltpu.VMEM((SD, PIX), BF16),
            pltpu.VMEM((4 * ROWS, SD), BF16),
            pltpu.VMEM((NS, ROWS, PIX), BF16),
            pltpu.VMEM((NS, ROWS, PIX), BF16),
            pltpu.VMEM((NS, 16, 128), BF16),
            pltpu.VMEM((NS, 16, 128), BF16),
            pltpu.VMEM((NF, NS, 16, 128), BF16),
            pltpu.VMEM((NF * NS, 16, 128), BF16),
            pltpu.VMEM((NS * 16, 128), F32),
            pltpu.VMEM((NG * 32, 1024), BF16),
            pltpu.VMEM((1024, 256), BF16),
            pltpu.VMEM((NG * 32, NPHI), BF16),
            pltpu.VMEM((1024, NPHI), F32),
            pltpu.VMEM((NJ, 8 * DET, PIX), BF16),
            pltpu.VMEM((NF, NS, 16, 128), BF16),
            pltpu.VMEM((NF * NS, 16, 128), BF16),
            pltpu.VMEM((128, 128), F32),
            pltpu.VMEM((SD, NF * NS * 16), BF16),
            pltpu.VMEM((256, LANES), BF16),
            pltpu.VMEM((16, 128), I32),
            dma((9,)), dma((NS,)), dma((NS,)), dma((NF * NS,)), dma((NF * NS,)), dma((NS,)), dma((NS,)),
            dma((2 * NG,)), dma((2 * NG,)), dma((NF * NS,)), dma((NF * NS,)),
        ],
        compiler_params=pltpu.CompilerParams(
            collective_id=0, has_side_effects=True, vmem_limit_bytes=65_500_000
        ),
    )(
        alm.reshape(alm.shape[0], 2, L), band_index, band_weight, legendre, orders.reshape(2, 128),
        owner.reshape(16, 128), tile_local.reshape(16, 128), interp, jnp.asarray(lane_table()),
    )
    return turned.T


def solution(mesh):
    placed = (
        P("freq", ("grp", "sub"), None, None),
        P(),
        P(),
        P(("grp", "sub"), None, None),
        P(),
        P(("grp", "sub"), None),
        P(("grp", "sub")),
        P(("grp", "sub"), None),
    )
    return jax.shard_map(
        on_device, mesh=mesh, in_specs=placed, out_specs=P(("grp", "sub"), "freq"), check_vma=False
    )
```

```python
import math

import jax
import jax.numpy as jnp
import numpy as np
from jax import lax
from jax.experimental import pallas as pl
from jax.experimental.pallas import tpu as pltpu
from jax.sharding import PartitionSpec as P

MESH = pl.DeviceIdType.MESH
F32, BF16, I32 = jnp.float32, jnp.bfloat16, jnp.int32
NF, NG, NS = 2, 16, 16
DET = 32
HALF_DET = DET // NF
L = 1024
RH = 512
NPHI = 1024
SD = 2048
PIX = 512
CAP = 12
NJ = 8
ROWS = NJ * CAP
GROUP = ROWS // 2
HALF_LANES = NS * GROUP
LANES = 2 * HALF_LANES
NN = (((1,), (0,)), ((), ()))
NT = (((1,), (1,)), ((), ()))
TN = (((0,), (0,)), ((), ()))


def dot(a, b, dims=NN):
    return lax.dot_general(a, b, dims, preferred_element_type=F32)


def lane_table():
    lane = np.arange(LANES)
    g, rest = lane // HALF_LANES, lane % HALF_LANES
    s, j4, k = rest // GROUP, rest % GROUP // CAP, rest % CAP
    table = np.zeros((8, LANES), np.int32)
    table[0] = s * NJ + g * 4 + j4
    table[1] = k
    table[2] = g * 4 + j4
    table[3] = s * 16 + k
    table[4] = j4 * 8
    return table


def kernel(
    alm_hbm, bidx_hbm, bwt_hbm, leg_ref, ord_hbm, own_hbm, tile_hbm, int_ref, tab_hbm, out_ref,
    alm_ref, bidx_ref, bwt_ref, ord_ref, own_ref, tile_ref, tab_ref, ordb_ref,
    leg_v, int_v, pick, d_s, d_r, t_s, t_r, y_s, y_r, y_f, coef, coef_t, basis, acc, tiles,
    v_s, v_r, cols, sel_v, sel_s, rank_v,
    loc_sem, ts_sem, tr_sem, ys_sem, yr_sem, ds_sem, dr_sem, rs_sem, rr_sem, vs_sem, vr_sem,
):
    f, z, s = lax.axis_index("freq"), lax.axis_index("grp"), lax.axis_index("sub")
    me = f * NS + s

    leg_copy = pltpu.make_async_copy(leg_ref.at[0], leg_v, loc_sem.at[0])
    int_copy = pltpu.make_async_copy(int_ref, int_v, loc_sem.at[1])
    small = [
        pltpu.make_async_copy(source, target, loc_sem.at[2 + n])
        for n, (source, target) in enumerate((
            (alm_hbm, alm_ref), (bidx_hbm, bidx_ref), (bwt_hbm, bwt_ref), (ord_hbm, ord_ref),
            (own_hbm, own_ref), (tile_hbm, tile_ref), (tab_hbm, tab_ref),
        ))
    ]
    for copy in small:
        copy.start()
    leg_copy.start()
    int_copy.start()

    barrier = pltpu.get_barrier_semaphore()

    def greet(k, _):
        other = lax.rem(me + k, NF * NS)
        pl.semaphore_signal(
            barrier, inc=1, device_id=(other // NS, z, lax.rem(other, NS)), device_id_type=MESH
        )
        return 0

    lax.fori_loop(1, NF * NS, greet, 0)
    for hops in (1, 2, NG - 2, NG - 1):
        pl.semaphore_signal(
            barrier, inc=1, device_id=(f, lax.rem(z + hops, NG), s), device_id_type=MESH
        )

    for copy in small:
        copy.wait()
    freqs = alm_ref.shape[0]
    freq = lax.broadcasted_iota(I32, (DET, freqs), 1) + f * freqs
    band = jnp.zeros((DET, freqs), F32)
    for k in range(bidx_ref.shape[1]):
        band = band + jnp.where(bidx_ref[:, k : k + 1] == freq, bwt_ref[:, k : k + 1], 0.0)
    band = band.astype(BF16)
    part = jnp.concatenate([dot(band, alm_ref[:, c, :]) for c in range(2)], axis=1)
    for h in range(2):
        spread_rows = jnp.broadcast_to(ord_ref[h : h + 1, :].astype(F32), (128, 128))
        ordb_ref[h * 128 : (h + 1) * 128, :] = spread_rows.T.astype(I32)

    degree = lax.rem(lax.broadcasted_iota(I32, (DET, 2 * L), 1), L)
    order = ordb_ref[pl.ds(z * NS + s, 1), :][:, :1]
    part = jnp.where(degree >= order, part, 0.0).astype(BF16)
    leg_copy.wait()
    cyc = dot(jnp.concatenate([part[:, :L], part[:, L:]], axis=0), leg_v[...])
    turn = lax.broadcasted_iota(I32, (DET, RH), 1) & 3
    quads = (
        lax.broadcasted_iota(I32, (128, RH), 1) // 4 == lax.broadcasted_iota(I32, (128, RH), 0)
    ).astype(BF16)
    for h in range(NF):
        pair = []
        for c in range(2):
            one = cyc[c * DET : (c + 1) * DET, h * RH : (h + 1) * RH]
            spread = jnp.concatenate([jnp.where(turn == i, one, 0.0) for i in range(4)], axis=0)
            pair.append(dot(quads, spread.astype(BF16), NT).reshape(NS, NJ, 128))
        y_s[h] = jnp.concatenate(pair, axis=1).astype(BF16)

    def y_copy(k, dst):
        other = lax.rem(me + k, NF * NS)
        oh, os = other // NS, lax.rem(other, NS)
        return pltpu.make_async_remote_copy(
            src_ref=y_s.at[oh, os], dst_ref=y_r.at[dst],
            send_sem=ys_sem.at[k], recv_sem=yr_sem.at[k],
            device_id=(oh, z, os), device_id_type=MESH,
        )

    def start_y(k, _):
        y_copy(k, me).start()
        return 0

    pl.semaphore_wait(barrier, NF * NS - 1 + 4)
    lax.fori_loop(1, NF * NS, start_y, 0)
    y_r[me] = y_s[f, s]

    lane = lax.broadcasted_iota(I32, (128, 128), 1)
    row = lax.broadcasted_iota(I32, (128, 128), 0)
    before = (row < lane).astype(BF16)
    band_row = lax.broadcasted_iota(I32, (NF * NS * NJ, 128), 0)
    rank_row = lax.broadcasted_iota(I32, (16, 128), 0)
    seen = jnp.zeros((NF * NS * NJ, 1), F32)
    slot_tile = jnp.zeros((16, NF * NS * NJ), F32)
    for c in range(SD // 128):
        named = band_row == own_ref[c : c + 1, :]
        ones = jnp.where(named, 1.0, 0.0)
        marks = ones.astype(BF16)
        count = dot(marks, before) + seen
        rank = jnp.sum(jnp.where(named, count, 0.0), axis=0, keepdims=True)
        seen = seen + jnp.sum(ones, axis=1, keepdims=True)
        rank_i = rank.astype(I32)
        rank_v[c : c + 1, :] = rank_i
        ids = jnp.where(rank_row == rank_i, tile_ref[c : c + 1, :].astype(F32), 0.0)
        slot_tile = slot_tile + dot(ids.astype(BF16), marks, NT)
    half_tile = jnp.where(f == 0, slot_tile[:, :128], slot_tile[:, 128:])
    lane16 = lax.broadcasted_iota(I32, (16, 128), 1)
    mine16 = lane16 // NJ == s

    def put_tiles(other, _):
        turned = pltpu.roll(half_tile, lax.rem(s - other + NS, NS) * NJ, 1)
        t_s[other] = jnp.where(mine16, turned, 0.0).astype(BF16)
        return 0

    lax.fori_loop(0, NS, put_tiles, 0)

    def t_copy(k, dst):
        return pltpu.make_async_remote_copy(
            src_ref=t_s.at[lax.rem(s + k, NS)], dst_ref=t_r.at[dst],
            send_sem=ts_sem.at[k], recv_sem=tr_sem.at[k],
            device_id=(f, z, lax.rem(s + k, NS)), device_id_type=MESH,
        )

    def d_copy(k, dst):
        return pltpu.make_async_remote_copy(
            src_ref=d_s.at[lax.rem(s + k, NS)], dst_ref=d_r.at[dst],
            send_sem=ds_sem.at[k], recv_sem=dr_sem.at[k],
            device_id=(f, z, lax.rem(s + k, NS)), device_id_type=MESH,
        )

    int_copy.wait()
    slot_row = lax.broadcasted_iota(I32, (ROWS, 128), 0)

    def pack(q, _):
        wanted = jnp.concatenate(
            [slot_row + lax.rem(s + q * 4 + n, NS) * ROWS for n in range(4)], axis=0
        )
        for c in range(SD // 128):
            key = (own_ref[c : c + 1, :] - f * 128) * CAP + rank_v[c : c + 1, :]
            pick[:, c * 128 : (c + 1) * 128] = jnp.where(wanted == key, 1.0, 0.0).astype(BF16)
        packed = dot(pick[...], int_v[...]).astype(BF16)
        for n in range(4):
            k = q * 4 + n
            d_s[lax.rem(s + k, NS)] = packed[n * ROWS : (n + 1) * ROWS, :]

            @pl.when(k > 0)
            def _(k=k):
                t_copy(k, s).start()
                d_copy(k, s).start()

        return 0

    lax.fori_loop(0, 2, pack, 0)
    t_r[s] = t_s[s]
    d_r[s] = d_s[s]

    def wait_y(k, _):
        y_copy(k, lax.rem(me + NF * NS - k, NF * NS)).wait_recv()
        return 0

    lax.fori_loop(1, NF * NS, wait_y, 0)
    y_f[...] = (y_r[0:NS].astype(F32) + y_r[NS : 2 * NS].astype(F32)).reshape(NS * 16, 128)
    for c in range(2):
        for j in range(NJ):
            coef[c * 16 : (c + 1) * 16, j * 128 : (j + 1) * 128] = y_f[
                pl.ds(c * NJ + j, NS, stride=16), :
            ].astype(BF16)

    def slot(d, way):
        return 0 if d == 0 else min(2 * d - (way == 0), NG - 1)

    def ring(d, hops, way, c):
        source, target = slot(d, way) * 32 + c * 16, slot(d + hops, way) * 32 + c * 16
        sem = slot(d + hops, way) * 2 + c
        return pltpu.make_async_remote_copy(
            src_ref=coef.at[pl.ds(source, 16), :], dst_ref=coef.at[pl.ds(target, 16), :],
            send_sem=rs_sem.at[sem], recv_sem=rr_sem.at[sem],
            device_id=(f, lax.rem(z + (hops if way == 0 else NG - hops), NG), s), device_id_type=MESH,
        )

    def ring_step(d):
        for hops in (2, 1):
            for c in range(2):
                for way in range(2):
                    if d > 0 and hops == 2:
                        ring(d - 2, 2, way, c).wait_recv()
                    if d + hops < 8 or way == c:
                        ring(d, hops, way, c).start()

    def ring_wait(*steps):
        for d, hops in steps:
            for c in range(2):
                for way in range(2):
                    if d + hops < 8 or way == c:
                        ring(d, hops, way, c).wait_recv()

    def sky_first(n, _):
        at = pl.ds(pl.multiple_of(n * 256, 256), 256)
        acc[:, at] = dot(coef_t[...], basis[0:256, at])
        return 0

    ring_step(0)
    lax.fori_loop(2, 4, pack, 0)

    def make_basis(p, _):
        hops = (p + 1) // 2
        zz = lax.rem(z + NG + (1 - 2 * lax.rem(p, 2)) * hops, NG)
        orders = ordb_ref[pl.ds(pl.multiple_of(zz * NS, NS), NS), :]
        lon = lax.broadcasted_iota(I32, (NS, 128), 1)
        fine = ((orders * lon) & (NPHI - 1)).astype(F32) * (2.0 * math.pi / NPHI)
        coarse = ((orders * (lon * 128)) & (NPHI - 1)).astype(F32) * (2.0 * math.pi / NPHI)
        weight = jnp.where(orders == 0, 1.0, 2.0)
        cos_u, sin_u = weight * jnp.cos(fine), weight * jnp.sin(fine)
        cos_t, sin_t = jnp.cos(coarse), jnp.sin(coarse)
        top = pl.multiple_of(p * 32, 32)
        for t in range(8):
            ct, st = cos_t[:, t : t + 1], sin_t[:, t : t + 1]
            basis[pl.ds(top, NS), t * 128 : (t + 1) * 128] = (ct * cos_u - st * sin_u).astype(BF16)
            basis[pl.ds(top + NS, NS), t * 128 : (t + 1) * 128] = (-(st * cos_u + ct * sin_u)).astype(BF16)
        return 0

    lax.fori_loop(0, NG, make_basis, 0)

    sel_s[...] = (lax.broadcasted_iota(I32, (256, LANES), 0) == tab_ref[3:4, :]).astype(BF16)
    cols[...] = jnp.zeros_like(cols)
    cols[0:16, :] = ((own_ref[...] // NJ) * 16 + rank_v[...]).astype(F32)
    cols[16:32, :] = (own_ref[...] & (NJ - 1)).astype(F32)
    turned_cols = cols[...].T
    place = lax.broadcasted_iota(I32, (128, NF * NS * 16), 1).astype(F32)
    for c in range(SD // 128):
        sel_v[c * 128 : (c + 1) * 128, :] = (place == turned_cols[:, c : c + 1]).astype(BF16)

    ring_step(2)
    ring_step(4)
    ring_wait((0, 1), (2, 1))
    coef_t[...] = coef[0:256, :].T
    lax.fori_loop(0, 2, sky_first, 0)
    ring_step(6)
    lax.fori_loop(2, 4, sky_first, 0)
    ring_wait((4, 1))
    coef_t[:, 0:128] = coef[256:384, :].T

    def wait_t(k, _):
        t_copy(k, lax.rem(s + NS - k, NS)).wait_recv()
        return 0

    lax.fori_loop(1, NS, wait_t, 0)
    tile_sum = jnp.sum(t_r[...].astype(F32), axis=0).astype(BF16)
    here = (lax.broadcasted_iota(I32, (128, LANES), 0) == tab_ref[0:1, :]).astype(BF16)
    by_rank = dot(tile_sum, here)
    own_rank = lax.broadcasted_iota(I32, (16, LANES), 0) == tab_ref[1:2, :]
    code = jnp.sum(jnp.where(own_rank, by_rank, 0.0), axis=0, keepdims=True).astype(I32)
    code = code + tab_ref[4:5, :]

    ring_wait((6, 2), (6, 1))

    def sky_last(n, _):
        at = pl.ds(pl.multiple_of(n * 256, 256), 256)
        sky = (acc[:, at] + dot(coef_t[...], basis[256:512, at])).astype(BF16)
        for h in range(2):
            to = pl.ds(pl.multiple_of((2 * n + h) * DET, DET), DET)
            for j in range(NJ):
                for i in range(4):
                    top = j * 128 + i * DET
                    tiles[j, to, i * 128 : (i + 1) * 128] = sky[
                        top : top + DET, h * 128 : (h + 1) * 128
                    ]
        return 0

    coef_t[:, 128:256] = coef[384:512, :].T
    lax.fori_loop(0, 4, sky_last, 0)

    def wait_d(k, _):
        d_copy(k, lax.rem(s + NS - k, NS)).wait_recv()
        return 0

    lax.fori_loop(1, NS, wait_d, 0)
    sums = []
    for g in range(2):
        weights = d_r[:, g * GROUP : (g + 1) * GROUP, :].reshape(HALF_LANES, PIX)
        pixels = tiles[g * 4 : (g + 1) * 4].reshape(4 * 8 * DET, PIX)
        for n in range(HALF_LANES // 256):
            every = dot(pixels, weights[n * 256 : (n + 1) * 256, :], NT)
            picked = code[:, g * HALF_LANES + n * 256 : g * HALF_LANES + (n + 1) * 256]
            value = jnp.zeros((DET, 256), F32)
            for t in range(32):
                value = value + jnp.where(picked == t, every[t * DET : (t + 1) * DET, :], 0.0)
            sums.append(value)
    value = jnp.concatenate(sums, axis=1)
    band = tab_ref[2:3, :]
    spread = jnp.concatenate(
        [
            jnp.where(band == j, value[h * HALF_DET : (h + 1) * HALF_DET, :], 0.0).astype(BF16)
            for h in range(NF)
            for j in range(NJ)
        ],
        axis=0,
    )
    together = dot(sel_s[...], spread, NT).astype(BF16)
    for h in range(NF):
        v_s[h] = together[:, h * 128 : (h + 1) * 128].reshape(NS, 16, 128)

    def v_copy(k, dst):
        other = lax.rem(me + k, NF * NS)
        oh, os = other // NS, lax.rem(other, NS)
        return pltpu.make_async_remote_copy(
            src_ref=v_s.at[oh, os], dst_ref=v_r.at[dst],
            send_sem=vs_sem.at[k], recv_sem=vr_sem.at[k],
            device_id=(oh, z, os), device_id_type=MESH,
        )

    def start_v(k, _):
        v_copy(k, me).start()
        return 0

    def wait_v(k, _):
        v_copy(k, lax.rem(me + NF * NS - k, NF * NS)).wait_recv()
        return 0

    lax.fori_loop(1, NF * NS, start_v, 0)
    v_r[me] = v_s[f, s]
    lax.fori_loop(1, NF * NS, wait_v, 0)

    found = dot(sel_v[...], v_r[...].reshape(NF * NS * 16, 128))
    fold = (rank_row == (lane16 & (HALF_DET - 1))).astype(BF16)
    lane_band = (lane // HALF_DET).astype(F32)
    for c in range(SD // 128):
        kept = jnp.where(
            lane_band == turned_cols[:, 16 + c : 17 + c], found[c * 128 : (c + 1) * 128, :], 0.0
        )
        out_ref[:, c * 128 : (c + 1) * 128] = dot(fold, kept.astype(BF16), NT).astype(BF16)

    def sent(k, _):
        t_copy(k, s).wait_send()
        d_copy(k, s).wait_send()
        return 0

    def sent_all(k, _):
        y_copy(k, me).wait_send()
        v_copy(k, me).wait_send()
        return 0

    lax.fori_loop(1, NS, sent, 0)
    lax.fori_loop(1, NF * NS, sent_all, 0)
    for d in range(0, 8, 2):
        for hops in (1, 2):
            for c in range(2):
                for way in range(2):
                    if d + hops < 8 or way == c:
                        ring(d, hops, way, c).wait_send()


def on_device(alm, band_index, band_weight, legendre, orders, owner, tile_local, interp):
    dma = pltpu.SemaphoreType.DMA
    vmem = pl.BlockSpec(memory_space=pltpu.VMEM)
    hbm = pl.BlockSpec(memory_space=pltpu.HBM)
    turned = pl.pallas_call(
        kernel,
        out_shape=jax.ShapeDtypeStruct((HALF_DET, SD), BF16),
        in_specs=[hbm] * 9,
        out_specs=vmem,
        scratch_shapes=[
            pltpu.VMEM((alm.shape[0], 2, L), BF16),
            pltpu.VMEM(band_index.shape, I32),
            pltpu.VMEM(band_weight.shape, F32),
            pltpu.VMEM((2, 128), I32),
            pltpu.VMEM((16, 128), I32),
            pltpu.VMEM((16, 128), I32),
            pltpu.VMEM((8, LANES), I32),
            pltpu.VMEM((256, 128), I32),
            pltpu.VMEM(legendre.shape[1:], BF16),
            pltpu.VMEM((SD, PIX), BF16),
            pltpu.VMEM((4 * ROWS, SD), BF16),
            pltpu.VMEM((NS, ROWS, PIX), BF16),
            pltpu.VMEM((NS, ROWS, PIX), BF16),
            pltpu.VMEM((NS, 16, 128), BF16),
            pltpu.VMEM((NS, 16, 128), BF16),
            pltpu.VMEM((NF, NS, 16, 128), BF16),
            pltpu.VMEM((NF * NS, 16, 128), BF16),
            pltpu.VMEM((NS * 16, 128), F32),
            pltpu.VMEM((NG * 32, 1024), BF16),
            pltpu.VMEM((1024, 256), BF16),
            pltpu.VMEM((NG * 32, NPHI), BF16),
            pltpu.VMEM((1024, NPHI), F32),
            pltpu.VMEM((NJ, 8 * DET, PIX), BF16),
            pltpu.VMEM((NF, NS, 16, 128), BF16),
            pltpu.VMEM((NF * NS, 16, 128), BF16),
            pltpu.VMEM((128, 128), F32),
            pltpu.VMEM((SD, NF * NS * 16), BF16),
            pltpu.VMEM((256, LANES), BF16),
            pltpu.VMEM((16, 128), I32),
            dma((9,)), dma((NS,)), dma((NS,)), dma((NF * NS,)), dma((NF * NS,)), dma((NS,)), dma((NS,)),
            dma((2 * NG,)), dma((2 * NG,)), dma((NF * NS,)), dma((NF * NS,)),
        ],
        compiler_params=pltpu.CompilerParams(
            collective_id=0, has_side_effects=True, vmem_limit_bytes=65_500_000
        ),
    )(
        alm.reshape(alm.shape[0], 2, L), band_index, band_weight, legendre, orders.reshape(2, 128),
        owner.reshape(16, 128), tile_local.reshape(16, 128), interp, jnp.asarray(lane_table()),
    )
    return turned.T


def solution(mesh):
    placed = (
        P("freq", ("grp", "sub"), None, None),
        P(),
        P(),
        P(("grp", "sub"), None, None),
        P(),
        P(("grp", "sub"), None),
        P(("grp", "sub")),
        P(("grp", "sub"), None),
    )
    return jax.shard_map(
        on_device, mesh=mesh, in_specs=placed, out_specs=P(("grp", "sub"), "freq"), check_vma=False
    )
```
